512 devices in a mesh: curve: 128 (over z, x, core), head: 4 (over y).
Axes of the slice: x: 4, y: 4, z: 16, core: 2. Of those that a mesh axis runs over, the one named last changes fastest.
Arguments:
- features: float32 [65536, 512], P('curve', 'head')
- input_proj: float32 [512, 3, 512], P(None, None, 'head')
- output_proj: float32 [512, 512], P('head'), may hold values from -0.25 to 0.25
- destination: int32 [65536], P('curve'), may hold values from 0 to 65535, as said below
- real_points: int32 [65536], P('curve'), may hold values from 0 to 1, as said below
- cotangent: float32 [65536, 512], P('curve', 'head'), may hold values from -6 to 6
Outputs:
- branch_out: float32 [65536, 512], P('curve', 'head')
- grad_features: float32 [65536, 512], P('curve', 'head')
- grad_inproj: float32 [512, 3, 512], P(None, None, 'head')
- grad_outproj: float32 [512, 512], P('head')
The draws below stay inside these ranges and needn't reach their ends.
Inputs may be any that keep to these rules, and one draw needn't show every extreme that they name: `destination`: A permutation of the points. Each aligned block of 512 points in the first order sends exactly 4 points to each aligned block of 512 positions in the second order. `real_points`: the first 128 points of every aligned block of 512 points are real.
All inputs are finite; a program needn't handle non-finite values.
Results may differ from the reference program's by a relative error of at most 0.0003.
Values sent between devices are 32-bit elements; how exact they have to be, the bound alone decides.
No kernel may reach another device: no remote copies, remote signals or barrier semaphores. Data moves between devices by JAX's collectives and lax.ppermute only.
A program may use at most 64 MiB of HBM per device.

```python
import math
import jax
import jax.numpy as jnp
from jax import lax

D = 512
HEADS = 16
PATCH = 512
PATCHES_DEV = 1
POINTS = 65536
N_CURVE = 128


def draw_features(key, part):
    key = jax.random.fold_in(key, 11)
    first = jax.random.fold_in(key, 0)
    total = PATCHES_DEV * PATCH * N_CURVE
    base = jax.random.normal(first, (total, D), jnp.float32)
    return base


def draw_input_proj(key, part):
    key = jax.random.fold_in(key, 17)
    base = jax.random.normal(key, (D, 3, D), jnp.float32) / math.sqrt(D)
    return base


def draw_destination(key, part):
    key = jax.random.fold_in(key, 23)
    row_count = PATCHES_DEV * PATCH
    per_peer = row_count // N_CURVE
    first, second = jax.random.split(key)
    sender = jax.vmap(lambda k: jax.random.permutation(k, row_count))(jax.random.split(first, N_CURVE))
    taker = jax.vmap(lambda k: jax.random.permutation(k, row_count))(jax.random.split(second, N_CURVE))
    slots = jnp.arange(row_count)
    blocks = slots // per_peer
    within = slots % per_peer
    source = jnp.arange(N_CURVE)[:, None]
    target = blocks[None, :] * row_count + taker[blocks[None, :], source * per_peer + within[None, :]]
    anchor = source * row_count + sender
    empty = jnp.zeros((N_CURVE * row_count,), jnp.int32)
    return empty.at[anchor.reshape(-1)].set(target.reshape(-1).astype(jnp.int32))


def draw_real_points(key, part):
    key = jax.random.fold_in(key, 31)
    row_count = PATCHES_DEV * PATCH
    first, second = jax.random.split(key)
    levels = jax.random.randint(first, (N_CURVE, 1), 1, 5)
    picks = jax.random.randint(second, (N_CURVE, row_count), 0, 4)
    live = (picks < levels).astype(jnp.int32)
    offset = jnp.arange(row_count) % PATCH
    live = jnp.where(offset[None, :] < PATCH // 4, 1, live).astype(jnp.int32)
    return live.reshape(-1)


def shard_levels(rng, dims, shards, low, high):
    def one(axis_at, shards_of):
        draws = jax.random.uniform(jax.random.fold_in(jax.random.fold_in(rng, 6), axis_at), (shards_of,), jnp.float32, low / len(shards), high / len(shards))
        return jnp.repeat(jnp.exp(draws), dims[axis_at] // shards_of).reshape((-1,) + (1,) * (len(dims) - axis_at - 1))

    factor_of = one(*shards[0])
    for cut in shards[1:]:
        factor_of = factor_of * one(*cut)
    return factor_of


def scatter_about(key, extent, width, bound, shards=(), kind=jnp.bfloat16):
    drawn = jax.random.normal(key, extent, jnp.float32) * width
    if len(shards) > 0:
        drawn = shard_levels(key, extent, shards, -0.22, 0.18) * drawn
    return jnp.clip(drawn, min=-bound, max=bound).astype(kind)


def setup_inputs(seed: int = 0) -> dict:
    streams_of = jax.random.split(jax.random.key(seed), 7)
    return {
        "features": draw_features(jax.random.fold_in(streams_of[6], 71), 0),
        "input_proj": draw_input_proj(jax.random.fold_in(streams_of[6], 71), 0),
        "output_proj": scatter_about(streams_of[2], (D, D), D ** -0.5, 0.25, ((0, 4),), jnp.float32),
        "destination": draw_destination(jax.random.fold_in(streams_of[6], 71), 0),
        "real_points": draw_real_points(jax.random.fold_in(streams_of[6], 71), 0),
        "cotangent": scatter_about(streams_of[5], (POINTS, D), 1.0, 6.0, ((0, 128), (1, 4)), jnp.float32),
    }


highest = lax.Precision.HIGHEST

def patch_attention(operands):
    block, validity = operands
    queries = block[:, 0]
    key_rows = block[:, 1]
    values = block[:, 2]
    scaling = 1.0 / math.sqrt(queries.shape[-1])
    scores = jnp.einsum('qhe,khe->hqk', queries, key_rows, precision=highest) * scaling
    scores = jnp.where(validity[None, None, :] > 0, scores, -jnp.inf)
    row_max = lax.optimization_barrier(jnp.max(scores, axis=-1, keepdims=True))
    weights = jnp.exp(scores - row_max)
    probability = weights / lax.optimization_barrier(jnp.sum(weights, axis=-1, keepdims=True))
    return jnp.einsum('hqk,khe->qhe', probability, values, precision=highest)

def forward(features, input_proj, output_proj, destination, real_points):
    total = features.shape[0]
    serial = jnp.zeros_like(features).at[destination].set(features)
    qkv = jnp.einsum('nd,dtf->ntf', serial, input_proj, precision=highest)
    qkv = jnp.roll(qkv, PATCH // 2, axis=0).reshape(total // PATCH, PATCH, 3, HEADS, D // HEADS)
    validity = jnp.roll(real_points, PATCH // 2).reshape(total // PATCH, PATCH)
    attended = lax.map(jax.checkpoint(patch_attention), (qkv, validity))
    attended = jnp.roll(attended.reshape(total, D), -(PATCH // 2), axis=0)
    return jnp.dot(attended, output_proj, precision=highest)

def reference(features, input_proj, output_proj, destination, real_points, cotangent):

    def closed(first, second, third):
        return forward(first, second, third, destination, real_points)
    branch_out, pullback = jax.vjp(closed, features, input_proj, output_proj)
    grad_features, grad_inproj, grad_outproj = pullback(cotangent)
    return (branch_out, grad_features, grad_inproj, grad_outproj)
```

```python
import functools
import math

import jax
import jax.numpy as jnp
from jax import lax
from jax.experimental import pallas as pl
from jax.experimental.pallas import tpu as pltpu
from jax.sharding import PartitionSpec as P

D = 512
HEADS = 16
PATCH = 512
HALF = PATCH // 2
HEAD = D // HEADS
WIDTH = 128
HERE = WIDTH // HEAD
CURVE = ("z", "x", "core")
BF = jnp.bfloat16
F32 = jnp.float32
SCALE = 1.0 / math.sqrt(HEAD)
LOG2E = math.log2(math.e)

NN = (((1,), (0,)), ((), ()))
NT = (((1,), (1,)), ((), ()))


def mm(a, b, dims=NN):
    return lax.dot_general(a, b, dims, preferred_element_type=F32)


def split(x):
    high = x.astype(BF)
    return high, (x - high.astype(F32)).astype(BF)


def split3(x):
    high, rest = x.astype(BF), None
    rest = x - high.astype(F32)
    mid = rest.astype(BF)
    return high, mid, (rest - mid.astype(F32)).astype(BF)


def mm3(a, b, dims=NN):
    (ah, al), (bh, bl) = a, b
    return mm(ah, bh, dims) + (mm(ah, bl, dims) + mm(al, bh, dims))


def select_rows(pick, x):
    high, mid, low = split3(x)
    return mm(pick, high) + (mm(pick, mid) + mm(pick, low))


def column(row):
    return jnp.transpose(jnp.broadcast_to(row, (WIDTH, PATCH)))


def wide(col):
    return jnp.concatenate([col] * (PATCH // WIDTH), axis=1)


def iota(dim):
    return lax.broadcasted_iota(jnp.int32, (PATCH, PATCH), dim).astype(F32)


def rows_to_slots(slot_row):
    return jnp.where(iota(0) == slot_row, 1.0, 0.0).astype(BF)


def slots_to_rows(slot_row):
    return jnp.where(wide(column(slot_row)) == iota(1), 1.0, 0.0).astype(BF)


def sort_kernel(each, dest_ref, feat_ref, sorted_ref, local_ref, slot_ref):
    dest = dest_ref[...]
    block = dest // PATCH
    local = (dest - block * PATCH).astype(F32)
    block = block.astype(F32)
    lower = iota(0) < iota(1)
    same = (wide(column(block)) == block) & lower
    rank = jnp.sum(jnp.where(same, 1.0, 0.0), axis=0, keepdims=True)
    slot = block * each + rank
    slot_ref[...] = slot
    back = wide(column(slot)) == iota(1)
    local_ref[...] = jnp.sum(jnp.where(back, wide(column(local)), 0.0), axis=0, keepdims=True)
    sorted_ref[...] = select_rows(rows_to_slots(slot), feat_ref[...])


def place_kernel(local_ref, arrived_ref, low_ref, high_ref):
    placed = select_rows(rows_to_slots(local_ref[...]), arrived_ref[...])
    low_ref[...] = placed[:HALF]
    high_ref[...] = placed[HALF:]


def unplace_kernel(local_ref, low_ref, high_ref, out_ref):
    grads = jnp.concatenate([low_ref[...], high_ref[...]], axis=0)
    out_ref[...] = select_rows(slots_to_rows(local_ref[...]), grads)


def unsort_kernel(slot_ref, returned_ref, out_ref):
    out_ref[...] = select_rows(slots_to_rows(slot_ref[...]), returned_ref[...])


def cot_kernel(cot_ref, wout_ref, grad_ref):
    total = jnp.zeros((PATCH, WIDTH), F32)
    for part in range(D // WIDTH):
        total += mm3(split(cot_ref[part]), split(wout_ref[:, part * WIDTH : (part + 1) * WIDTH]), NT)
    grad_ref[...] = total


def head_mask(head):
    lanes = lax.broadcasted_iota(jnp.int32, (PATCH, WIDTH), 1)
    return (lanes // HEAD) == head


def scores_of(queries, key_rows, mask):
    qh, ql = split(queries)
    kh, kl = split(jnp.where(mask, key_rows, 0.0))
    keys = jnp.concatenate([kh, kl], axis=1)
    return mm(keys, jnp.concatenate([qh, qh], axis=1), NT) + mm(
        keys, jnp.concatenate([ql, ql], axis=1), NT
    )


def forward_kernel(x_ref, win_ref, wout_ref, bias_ref, qkv_ref, att_ref, lse_ref, out_ref, vt_ref):
    parts = [split(x_ref[part]) for part in range(D // WIDTH)]
    for t in range(3):
        total = jnp.zeros((PATCH, WIDTH), F32)
        for part in range(D // WIDTH):
            total += mm3(parts[part], split(win_ref[t, part * WIDTH : (part + 1) * WIDTH]))
        qkv_ref[t] = total
    vt_ref[...] = jnp.transpose(qkv_ref[2])
    bias = wide(bias_ref[...])

    def one(head, carry):
        mask = head_mask(head)
        scores = scores_of(qkv_ref[0] * (SCALE * LOG2E), qkv_ref[1], mask) + bias
        top = jnp.max(scores, axis=0, keepdims=True)
        weights = jnp.exp2(scores - top)
        total = jnp.sum(weights, axis=0, keepdims=True)
        rows = pl.ds(pl.multiple_of(head * HEAD, HEAD), HEAD)
        vh, vl = split(vt_ref[rows, :])
        wh, wl = split(weights)
        both = mm(jnp.concatenate([vh, vl], axis=0), wh)
        attended = both[:HEAD] + both[HEAD:] + mm(vh, wl)
        att_ref[rows, :] = attended / total
        lse_ref[pl.ds(head, 1), :] = top + jnp.log2(total)
        return carry

    lax.fori_loop(0, HERE, one, 0)
    attended = split(jnp.transpose(att_ref[...]))
    for part in range(D // WIDTH):
        out_ref[part] = mm3(attended, split(wout_ref[:, part * WIDTH : (part + 1) * WIDTH]))


def backward_kernel(qkv_ref, att_ref, lse_ref, grad_ref, bias_ref, dqkv_ref, kt_ref, gt_ref, dqt_ref):
    kt_ref[...] = jnp.transpose(qkv_ref[1])
    gt_ref[...] = jnp.transpose(grad_ref[...])
    bias = wide(bias_ref[...])
    dqkv_ref[1] = jnp.zeros((PATCH, WIDTH), F32)
    dqkv_ref[2] = jnp.zeros((PATCH, WIDTH), F32)

    def one(head, carry):
        mask = head_mask(head)
        rows = pl.ds(pl.multiple_of(head * HEAD, HEAD), HEAD)
        scores = scores_of(qkv_ref[0] * (SCALE * LOG2E), qkv_ref[1], mask) + bias
        probs = jnp.exp2(scores - lse_ref[pl.ds(head, 1), :])
        ph, plo = split(probs)
        grad_probs = scores_of(grad_ref[...], qkv_ref[2], mask)
        gh, gl = split(jnp.where(mask, grad_ref[...], 0.0))
        both = mm(ph, jnp.concatenate([gh, gl], axis=1))
        dqkv_ref[2] += both[:, :WIDTH] + both[:, WIDTH:] + mm(plo, gh)
        inner = jnp.sum(gt_ref[rows, :] * att_ref[rows, :], axis=0, keepdims=True)
        grad_scores = probs * (grad_probs - inner)
        sh, sl = split(grad_scores)
        qh, ql = split(jnp.where(mask, qkv_ref[0] * SCALE, 0.0))
        both = mm(sh, jnp.concatenate([qh, ql], axis=1))
        dqkv_ref[1] += both[:, :WIDTH] + both[:, WIDTH:] + mm(sl, qh)
        kh, kl = split(kt_ref[rows, :] * SCALE)
        both = mm(jnp.concatenate([kh, kl], axis=0), sh)
        dqt_ref[rows, :] = both[:HEAD] + both[HEAD:] + mm(kh, sl)
        return carry

    lax.fori_loop(0, HERE, one, 0)
    dqkv_ref[0] = jnp.transpose(dqt_ref[...])


def weights_kernel(x_ref, dqkv_ref, att_ref, cot_ref, din_ref, dout_ref):
    attended = split(att_ref[...])
    for part in range(D // WIDTH):
        dout_ref[part] = mm3(attended, split(cot_ref[part]))
    parts = [split(x_ref[part]) for part in range(D // WIDTH)]
    for t in range(3):
        grads = split(jnp.transpose(dqkv_ref[t]))
        for part in range(D // WIDTH):
            din_ref[t, part * WIDTH : (part + 1) * WIDTH] = jnp.transpose(mm3(grads, parts[part]))


def rows_kernel(dqkv_ref, win_ref, dx_ref):
    grads = [split(dqkv_ref[t]) for t in range(3)]
    for part in range(D // WIDTH):
        total = jnp.zeros((PATCH, WIDTH), F32)
        for t in range(3):
            total += mm3(grads[t], split(win_ref[t, part * WIDTH : (part + 1) * WIDTH]), NT)
        dx_ref[part] = total


def call(kernel, outs, *args, scratch=(), flops=10**9):
    size = sum(math.prod(a.shape) * 4 for a in (*args, *outs))
    return pl.pallas_call(
        kernel,
        out_shape=tuple(jax.ShapeDtypeStruct(o, F32) for o in [x.shape for x in outs]),
        in_specs=[pl.BlockSpec(memory_space=pltpu.VMEM)] * len(args),
        out_specs=tuple(pl.BlockSpec(memory_space=pltpu.VMEM) for _ in outs),
        scratch_shapes=[pltpu.VMEM(s, F32) for s in scratch],
        compiler_params=pltpu.CompilerParams(vmem_limit_bytes=40 * 2**20),
        cost_estimate=pl.CostEstimate(flops=flops, bytes_accessed=size, transcendentals=0),
    )(*args)


def of(*shape):
    return jax.ShapeDtypeStruct(shape, F32)


def gather_head(x):
    return lax.all_gather(x, "head", axis=0)


def scatter_head(x):
    return lax.psum_scatter(x, "head", scatter_dimension=0)


def total_over_curve(x):
    for axis in CURVE[::-1]:
        x = lax.psum_scatter(x, axis, scatter_dimension=0, tiled=True)
    for axis in CURVE:
        x = lax.all_gather(x, axis, axis=0, tiled=True)
    return x


def shards(features, input_proj, output_proj, destination, real_points, cotangent):
    peers = lax.axis_size(CURVE)
    up = [(i, (i + 1) % peers) for i in range(peers)]
    down = [(j, i) for i, j in up]

    def exchange(x):
        return lax.all_to_all(x, CURVE, split_axis=0, concat_axis=0, tiled=True)

    def to_patch(low, high):
        return jnp.concatenate([lax.ppermute(high, CURVE, up), low], axis=0)

    def from_patch(x):
        return x[HALF:], lax.ppermute(x[:HALF], CURVE, down)

    sorted_rows, local, slot = call(
        functools.partial(sort_kernel, PATCH // peers), [of(PATCH, WIDTH), of(1, PATCH), of(1, PATCH)],
        destination.reshape(1, PATCH), features,
    )
    local = exchange(local.reshape(PATCH)).reshape(1, PATCH)
    arrived = exchange(sorted_rows)
    win = jnp.transpose(input_proj, (1, 0, 2))
    cot = gather_head(to_patch(cotangent[:HALF], cotangent[HALF:]))
    valid = to_patch(real_points[:HALF], real_points[HALF:])
    bias = jnp.broadcast_to(jnp.where(valid > 0, 0.0, -jnp.inf).astype(F32)[:, None], (PATCH, WIDTH))
    (grad_attended,) = call(cot_kernel, [of(PATCH, WIDTH)], cot, output_proj)
    low, high = call(place_kernel, [of(HALF, WIDTH)] * 2, local, arrived)
    x = gather_head(to_patch(low, high))
    qkv, attended, lse, out = call(
        forward_kernel,
        [of(3, PATCH, WIDTH), of(WIDTH, PATCH), of(HERE, PATCH), of(D // WIDTH, PATCH, WIDTH)],
        x, win, output_proj, bias, scratch=[(WIDTH, PATCH)],
    )
    branch_out = jnp.concatenate(from_patch(scatter_head(out)), axis=0)
    (dqkv,) = call(
        backward_kernel, [of(3, PATCH, WIDTH)], qkv, attended, lse, grad_attended, bias,
        scratch=[(WIDTH, PATCH)] * 3,
    )
    (dx,) = call(rows_kernel, [of(D // WIDTH, PATCH, WIDTH)], dqkv, win)
    din, dout = call(
        weights_kernel, [of(3, D, WIDTH), of(D // WIDTH, WIDTH, WIDTH)], x, dqkv, attended, cot
    )
    low, high = from_patch(scatter_head(dx))
    (back,) = call(unplace_kernel, [of(PATCH, WIDTH)], local, low, high)
    (grad_features,) = call(unsort_kernel, [of(PATCH, WIDTH)], slot, exchange(back))
    both = jnp.concatenate([din.reshape(3 * D, WIDTH), dout.reshape(D, WIDTH)], axis=0)
    both = total_over_curve(both)
    grad_inproj = jnp.transpose(both[: 3 * D].reshape(3, D, WIDTH), (1, 0, 2))
    grad_outproj = jnp.transpose(both[3 * D :].reshape(D // WIDTH, WIDTH, WIDTH), (1, 0, 2)).reshape(WIDTH, D)
    return (branch_out, grad_features, grad_inproj, grad_outproj)


def solution(mesh):
    curve, head = mesh.devices.shape
    sizes = (curve // 8, 4, 2) if curve >= 16 else (curve // 2, 1, 2)
    fine = jax.sharding.Mesh(mesh.devices.reshape(*sizes, head), CURVE + ("head",))
    return jax.shard_map(
        shards,
        mesh=fine,
        in_specs=(
            P(CURVE, "head"),
            P(None, None, "head"),
            P("head", None),
            P(CURVE),
            P(CURVE),
            P(CURVE, "head"),
        ),
        out_specs=(P(CURVE, "head"), P(CURVE, "head"), P(None, None, "head"), P("head", None)),
        check_vma=False,
    )
```

```python
import functools
import math

import jax
import jax.numpy as jnp
from jax import lax
from jax.experimental import pallas as pl
from jax.experimental.pallas import tpu as pltpu
from jax.sharding import PartitionSpec as P

D = 512
HEADS = 16
PATCH = 512
HALF = PATCH // 2
HEAD = D // HEADS
WIDTH = 128
HERE = WIDTH // HEAD
CURVE = ("z", "x", "core")
BF = jnp.bfloat16
F32 = jnp.float32
SCALE = 1.0 / math.sqrt(HEAD)
LOG2E = math.log2(math.e)

NN = (((1,), (0,)), ((), ()))
NT = (((1,), (1,)), ((), ()))


def mm(a, b, dims=NN):
    return lax.dot_general(a, b, dims, preferred_element_type=F32)


def split(x):
    high = x.astype(BF)
    return high, (x - high.astype(F32)).astype(BF)


def split3(x):
    high, rest = x.astype(BF), None
    rest = x - high.astype(F32)
    mid = rest.astype(BF)
    return high, mid, (rest - mid.astype(F32)).astype(BF)


def mm3(a, b, dims=NN):
    (ah, al), (bh, bl) = a, b
    return mm(ah, bh, dims) + (mm(ah, bl, dims) + mm(al, bh, dims))


def select_rows(pick, x):
    high, mid, low = split3(x)
    return mm(pick, high) + (mm(pick, mid) + mm(pick, low))


def column(row):
    return jnp.transpose(jnp.broadcast_to(row, (WIDTH, row.shape[1])))


def wide(col, width=PATCH):
    return jnp.concatenate([col] * (width // WIDTH), axis=1)


def iota(dim, shape=(PATCH, PATCH)):
    return lax.broadcasted_iota(jnp.int32, shape, dim).astype(F32)


def one_hot(condition):
    return jnp.where(condition, 1.0, 0.0).astype(BF)


def spread(each, rows, arrived):
    total = arrived.shape[0]
    place = iota(0, (rows, total))
    peer = jnp.floor((place + 0.5) * (1.0 / each))
    pick = one_hot(iota(1, (rows, total)) == peer * (each + 1) + each)
    high, low = split(arrived)
    listed = mm(pick, high) + mm(pick, low)
    place = iota(0, (rows, WIDTH))
    turn = place - jnp.floor((place + 0.5) * (1.0 / each)) * each
    mine = jnp.where(iota(1, (rows, WIDTH)) == turn, listed, 0.0)
    return jnp.broadcast_to(jnp.sum(mine, axis=1, keepdims=True), (rows, WIDTH))


def sort_kernel(each, dest_ref, feat_ref, message_ref, slot_ref):
    dest = dest_ref[...]
    block = dest // PATCH
    local = (dest - block * PATCH).astype(F32)
    block = block.astype(F32)
    same = (wide(column(block)) == block) & (iota(0) < iota(1))
    rank = jnp.sum(jnp.where(same, 1.0, 0.0), axis=0, keepdims=True)
    slot_ref[...] = block * each + rank
    shape = (message_ref.shape[0], PATCH)
    rows = iota(0, shape)
    first = block * (each + 1)
    lists = jnp.where(iota(1, (PATCH, WIDTH)) == column(rank), column(local), 0.0)
    high, low = split(lists)
    last = one_hot(rows == first + each)
    message = select_rows(one_hot(rows == first + rank), feat_ref[...])
    message_ref[...] = message + (mm(last, high) + mm(last, low))


def positions_kernel(each, arrived_ref, position_ref):
    position_ref[...] = spread(each, PATCH, arrived_ref[...])


def place_kernel(each, arrived_ref, low_ref, high_ref):
    arrived = arrived_ref[...]
    total = arrived.shape[0]
    place = iota(0, (total, total))
    peer = jnp.floor((place + 0.5) * (1.0 / (each + 1)))
    pick = one_hot(iota(1, (total, total)) == peer * (each + 1) + each)
    high, low = split(arrived)
    listed = mm(pick, high) + mm(pick, low)
    place = iota(0, (total, WIDTH))
    turn = place - jnp.floor((place + 0.5) * (1.0 / (each + 1))) * (each + 1)
    mine = jnp.where((iota(1, (total, WIDTH)) == turn) & (turn < each), listed, 0.0)
    mine = jnp.sum(mine, axis=1, keepdims=True) - jnp.where(turn < each, 0.0, 1.0)
    row = jnp.transpose(jnp.broadcast_to(mine, (total, WIDTH)))[:1]
    placed = select_rows(one_hot(iota(0, (PATCH, total)) == row), arrived)
    low_ref[...] = placed[:HALF]
    high_ref[...] = placed[HALF:]


def add_kernel(parts_ref, total_ref):
    total_ref[...] = parts_ref[0] + parts_ref[1] + (parts_ref[2] + parts_ref[3])


def unplace_kernel(position_ref, low_ref, high_ref, out_ref):
    low = low_ref[0] + low_ref[1] + (low_ref[2] + low_ref[3])
    grads = jnp.concatenate([low, high_ref[...]], axis=0)
    out_ref[...] = select_rows(one_hot(wide(position_ref[...]) == iota(1)), grads)


def unsort_kernel(slot_ref, returned_ref, out_ref):
    pick = one_hot(wide(column(slot_ref[...])) == iota(1))
    out_ref[...] = select_rows(pick, returned_ref[...])


def cot_kernel(cot_ref, wout_ref, low_ref, high_ref):
    total = jnp.zeros((PATCH, WIDTH), F32)
    for part in range(D // WIDTH):
        total += mm3(split(cot_ref[part]), split(wout_ref[:, part * WIDTH : (part + 1) * WIDTH]), NT)
    low_ref[...] = total[:HALF]
    high_ref[...] = total[HALF:]


def head_mask(head):
    lanes = lax.broadcasted_iota(jnp.int32, (PATCH, WIDTH), 1)
    return (lanes // HEAD) == head


def scores_of(queries, key_rows, mask):
    qh, ql = split(queries)
    kh, kl = split(jnp.where(mask, key_rows, 0.0))
    keys = jnp.concatenate([kh, kl], axis=1)
    return mm(keys, jnp.concatenate([qh, qh], axis=1), NT) + mm(
        keys, jnp.concatenate([ql, ql], axis=1), NT
    )


def forward_kernel(x_ref, win_ref, bias_ref, qkv_ref, att_ref, lse_ref, early_ref, late_ref, vt_ref):
    parts = [split(x_ref[part]) for part in range(D // WIDTH)]
    for t in range(3):
        total = jnp.zeros((PATCH, WIDTH), F32)
        for part in range(D // WIDTH):
            total += mm3(parts[part], split(win_ref[t, part * WIDTH : (part + 1) * WIDTH]))
        qkv_ref[t] = total
    vt_ref[...] = jnp.transpose(qkv_ref[2])
    bias = wide(bias_ref[...])

    def one(head, carry):
        mask = head_mask(head)
        scores = scores_of(qkv_ref[0] * (SCALE * LOG2E), qkv_ref[1], mask) + bias
        top = jnp.max(scores, axis=0, keepdims=True)
        weights = jnp.exp2(scores - top)
        total = jnp.sum(weights, axis=0, keepdims=True)
        rows = pl.ds(pl.multiple_of(head * HEAD, HEAD), HEAD)
        vh, vl = split(vt_ref[rows, :])
        wh, wl = split(weights)
        both = mm(jnp.concatenate([vh, vl], axis=0), wh)
        attended = both[:HEAD] + both[HEAD:] + mm(vh, wl)
        att_ref[rows, :] = attended / total
        lse_ref[pl.ds(head, 1), :] = top + jnp.log2(total)
        return carry

    lax.fori_loop(0, HERE, one, 0)
    late_ref[...] = jnp.transpose(att_ref[:, HALF:])
    early_ref[...] = jnp.transpose(att_ref[:, :HALF])


def backward_kernel(qkv_ref, att_ref, lse_ref, grad_ref, bias_ref, dqkv_ref, kt_ref, gt_ref, dqt_ref):
    kt_ref[...] = jnp.transpose(qkv_ref[1])
    gt_ref[...] = jnp.transpose(grad_ref[...])
    bias = wide(bias_ref[...])
    dqkv_ref[1] = jnp.zeros((PATCH, WIDTH), F32)
    dqkv_ref[2] = jnp.zeros((PATCH, WIDTH), F32)

    def one(head, carry):
        mask = head_mask(head)
        rows = pl.ds(pl.multiple_of(head * HEAD, HEAD), HEAD)
        scores = scores_of(qkv_ref[0] * (SCALE * LOG2E), qkv_ref[1], mask) + bias
        probs = jnp.exp2(scores - lse_ref[pl.ds(head, 1), :])
        ph, plo = split(probs)
        grad_probs = scores_of(grad_ref[...], qkv_ref[2], mask)
        gh, gl = split(jnp.where(mask, grad_ref[...], 0.0))
        both = mm(ph, jnp.concatenate([gh, gl], axis=1))
        dqkv_ref[2] += both[:, :WIDTH] + both[:, WIDTH:] + mm(plo, gh)
        inner = jnp.sum(gt_ref[rows, :] * att_ref[rows, :], axis=0, keepdims=True)
        grad_scores = probs * (grad_probs - inner)
        sh, sl = split(grad_scores)
        qh, ql = split(jnp.where(mask, qkv_ref[0] * SCALE, 0.0))
        both = mm(sh, jnp.concatenate([qh, ql], axis=1))
        dqkv_ref[1] += both[:, :WIDTH] + both[:, WIDTH:] + mm(sl, qh)
        kh, kl = split(kt_ref[rows, :] * SCALE)
        both = mm(jnp.concatenate([kh, kl], axis=0), sh)
        dqt_ref[rows, :] = both[:HEAD] + both[HEAD:] + mm(kh, sl)
        return carry

    lax.fori_loop(0, HERE, one, 0)
    dqkv_ref[0] = jnp.transpose(dqt_ref[...])


def output_kernel(low_ref, high_ref, wout_ref, cot_ref, out_ref, dout_ref):
    attended = jnp.concatenate([low_ref[...], high_ref[...]], axis=0)
    parts = split(attended)
    turned = split(jnp.transpose(attended))
    for part in range(D // WIDTH):
        out_ref[part] = mm3(parts, split(wout_ref[:, part * WIDTH : (part + 1) * WIDTH]))
        dout_ref[part] = mm3(turned, split(cot_ref[part]))


def weights_kernel(x_ref, dqkv_ref, din_ref):
    parts = [split(x_ref[part]) for part in range(D // WIDTH)]
    for t in range(3):
        grads = split(jnp.transpose(dqkv_ref[t]))
        for part in range(D // WIDTH):
            din_ref[t, part * WIDTH : (part + 1) * WIDTH] = jnp.transpose(mm3(grads, parts[part]))


def rows_kernel(dqkv_ref, win_ref, dx_ref):
    grads = [split(dqkv_ref[t]) for t in range(3)]
    for part in range(D // WIDTH):
        total = jnp.zeros((PATCH, WIDTH), F32)
        for t in range(3):
            total += mm3(grads[t], split(win_ref[t, part * WIDTH : (part + 1) * WIDTH]), NT)
        dx_ref[part] = total


def call(kernel, outs, *args, scratch=(), flops=10**9):
    size = sum(math.prod(a.shape) * 4 for a in (*args, *outs))
    return pl.pallas_call(
        kernel,
        out_shape=tuple(jax.ShapeDtypeStruct(o, F32) for o in [x.shape for x in outs]),
        in_specs=[pl.BlockSpec(memory_space=pltpu.VMEM)] * len(args),
        out_specs=tuple(pl.BlockSpec(memory_space=pltpu.VMEM) for _ in outs),
        scratch_shapes=[pltpu.VMEM(s, F32) for s in scratch],
        compiler_params=pltpu.CompilerParams(vmem_limit_bytes=40 * 2**20),
        cost_estimate=pl.CostEstimate(flops=flops, bytes_accessed=size, transcendentals=0),
    )(*args)


def of(*shape):
    return jax.ShapeDtypeStruct(shape, F32)


def swap(x, axis):
    return lax.all_to_all(x, axis, split_axis=0, concat_axis=0, tiled=True)


def spread_to(x, axis):
    peers = lax.axis_size(axis)
    return swap(jnp.broadcast_to(x[None], (peers,) + x.shape).reshape(-1, WIDTH), axis)


def total_over_curve(x):
    for axis in CURVE[::-1]:
        peers = lax.axis_size(axis)
        x = jnp.sum(swap(x, axis).reshape(peers, -1, WIDTH), axis=0)
    for axis in CURVE:
        x = spread_to(x, axis)
    return x


def shards(features, input_proj, output_proj, destination, real_points, cotangent):
    peers = lax.axis_size(CURVE)
    each = PATCH // peers
    message_rows = PATCH + peers
    up = [(i, (i + 1) % peers) for i in range(peers)]
    down = [(j, i) for i, j in up]

    def to_patch(low, high):
        return jnp.concatenate([lax.ppermute(high, CURVE, up), low], axis=0)

    cot = lax.all_gather(cotangent, "head", axis=0)
    message, slot = call(
        functools.partial(sort_kernel, each), [of(message_rows, WIDTH), of(1, PATCH)],
        destination.reshape(1, PATCH), features,
    )
    arrived = swap(message.reshape(message_rows, 1, WIDTH), CURVE).reshape(message_rows, WIDTH)
    win = jnp.transpose(input_proj, (1, 0, 2))
    valid = to_patch(real_points[:HALF], real_points[HALF:])
    bias = jnp.broadcast_to(jnp.where(valid > 0, 0.0, -jnp.inf).astype(F32)[:, None], (PATCH, WIDTH))
    grad_low, grad_high = call(cot_kernel, [of(HALF, WIDTH)] * 2, cot, output_proj)
    grad_attended = to_patch(grad_low, grad_high)
    low, high = call(functools.partial(place_kernel, each), [of(HALF, WIDTH)] * 2, arrived)
    (position,) = call(functools.partial(positions_kernel, each), [of(PATCH, WIDTH)], arrived)
    x = spread_to(to_patch(low, high), "head").reshape(D // WIDTH, PATCH, WIDTH)
    qkv, attended, lse, early, late = call(
        forward_kernel,
        [of(3, PATCH, WIDTH), of(WIDTH, PATCH), of(HERE, PATCH), of(HALF, WIDTH), of(HALF, WIDTH)],
        x, win, bias, scratch=[(WIDTH, PATCH)],
    )
    (dqkv,) = call(
        backward_kernel, [of(3, PATCH, WIDTH)], qkv, attended, lse, grad_attended, bias,
        scratch=[(WIDTH, PATCH)] * 3,
    )
    out, dout = call(
        output_kernel, [of(D // WIDTH, PATCH, WIDTH), of(D // WIDTH, WIDTH, WIDTH)],
        late, lax.ppermute(early, CURVE, down), output_proj, cot,
    )
    branch_out = lax.psum_scatter(out, "head", scatter_dimension=0)
    (dx,) = call(rows_kernel, [of(D // WIDTH, PATCH, WIDTH)], dqkv, win)
    (din,) = call(weights_kernel, [of(3, D, WIDTH)], x, dqkv)
    dx = swap(dx.reshape(-1, WIDTH), "head").reshape(D // WIDTH, PATCH, WIDTH)
    (early,) = call(add_kernel, [of(HALF, WIDTH)], dx[:, :HALF])
    (back,) = call(
        unplace_kernel, [of(PATCH, WIDTH)], position, dx[:, HALF:], lax.ppermute(early, CURVE, down)
    )
    (grad_features,) = call(unsort_kernel, [of(PATCH, WIDTH)], slot, swap(back, CURVE))
    both = jnp.concatenate([din.reshape(3 * D, WIDTH), dout.reshape(D, WIDTH)], axis=0)
    both = total_over_curve(both)
    grad_inproj = jnp.transpose(both[: 3 * D].reshape(3, D, WIDTH), (1, 0, 2))
    grad_outproj = jnp.transpose(both[3 * D :].reshape(D // WIDTH, WIDTH, WIDTH), (1, 0, 2)).reshape(WIDTH, D)
    return (branch_out, grad_features, grad_inproj, grad_outproj)


def solution(mesh):
    curve, head = mesh.devices.shape
    sizes = (curve // 8, 4, 2) if curve >= 16 else (curve // 2, 1, 2)
    fine = jax.sharding.Mesh(mesh.devices.reshape(*sizes, head), CURVE + ("head",))
    return jax.shard_map(
        shards,
        mesh=fine,
        in_specs=(
            P(CURVE, "head"),
            P(None, None, "head"),
            P("head", None),
            P(CURVE),
            P(CURVE),
            P(CURVE, "head"),
        ),
        out_specs=(P(CURVE, "head"), P(CURVE, "head"), P(None, None, "head"), P("head", None)),
        check_vma=False,
    )
```

```python
import functools
import math

import jax
import jax.numpy as jnp
from jax import lax
from jax.experimental import pallas as pl
from jax.experimental.pallas import tpu as pltpu
from jax.sharding import PartitionSpec as P

D = 512
HEADS = 16
PATCH = 512
HALF = PATCH // 2
HEAD = D // HEADS
WIDTH = 128
HERE = WIDTH // HEAD
CURVE = ("far", "near", "x", "core")
PLANE = ("near", "x")
BLOCKS = 16
SIDE = WIDTH // 2
ADDED = 2
BF = jnp.bfloat16
F32 = jnp.float32
SCALE = 1.0 / math.sqrt(HEAD)
LOG2E = math.log2(math.e)

NN = (((1,), (0,)), ((), ()))
NT = (((1,), (1,)), ((), ()))


def mm(a, b, dims=NN):
    return lax.dot_general(a, b, dims, preferred_element_type=F32)


def split(x):
    high = x.astype(BF)
    return high, (x - high.astype(F32)).astype(BF)


def split3(x):
    high, rest = x.astype(BF), None
    rest = x - high.astype(F32)
    mid = rest.astype(BF)
    return high, mid, (rest - mid.astype(F32)).astype(BF)


def mm3(a, b, dims=NN):
    (ah, al), (bh, bl) = a, b
    return mm(ah, bh, dims) + (mm(ah, bl, dims) + mm(al, bh, dims))


def select_rows(pick, x):
    high, mid, low = split3(x)
    return mm(pick, high) + (mm(pick, mid) + mm(pick, low))


def column(row):
    return jnp.transpose(jnp.broadcast_to(row, (WIDTH, row.shape[1])))


def wide(col, width=PATCH):
    return jnp.concatenate([col] * (width // WIDTH), axis=1)


def iota(dim, shape=(PATCH, PATCH)):
    return lax.broadcasted_iota(jnp.int32, shape, dim).astype(F32)


def one_hot(condition):
    return jnp.where(condition, 1.0, 0.0).astype(BF)


def spread(each, size, rows, arrived):
    total = arrived.shape[0]
    place = iota(0, (rows, total))
    peer = jnp.floor((place + 0.5) * (1.0 / size))
    pick = one_hot(iota(1, (rows, total)) == peer * (each + 1) + each)
    high, low = split(arrived)
    listed = mm(pick, high) + mm(pick, low)
    place = iota(0, (rows, WIDTH))
    turn = place - jnp.floor((place + 0.5) * (1.0 / size)) * size
    mine = jnp.where((iota(1, (rows, WIDTH)) == turn) & (turn < each), listed, 0.0)
    mine = jnp.sum(mine, axis=1, keepdims=True)
    return jnp.where(turn < each, mine, -1.0)


def sort_kernel(each, dest_ref, feat_ref, message_ref, slot_ref):
    dest = dest_ref[...]
    block = dest // PATCH
    local = (dest - block * PATCH).astype(F32)
    block = block.astype(F32)
    same = (wide(column(block)) == block) & (iota(0) < iota(1))
    rank = jnp.sum(jnp.where(same, 1.0, 0.0), axis=0, keepdims=True)
    slot_ref[...] = block * each + rank
    shape = (message_ref.shape[0], PATCH)
    rows = iota(0, shape)
    first = block * (each + 1)
    lists = jnp.where(iota(1, (PATCH, WIDTH)) == column(rank), column(local), 0.0)
    high, low = split(lists)
    last = one_hot(rows == first + each)
    message = select_rows(one_hot(rows == first + rank), feat_ref[...])
    message_ref[...] = message + (mm(last, high) + mm(last, low))


def positions_kernel(each, arrived_ref, position_ref):
    position_ref[...] = spread(each, each + ADDED, position_ref.shape[0], arrived_ref[...])


def place_kernel(each, arrived_ref, low_ref, high_ref):
    arrived = arrived_ref[...]
    total = arrived.shape[0]
    row = jnp.transpose(spread(each, each + 1, total, arrived))[:1]
    placed = select_rows(one_hot(iota(0, (PATCH, total)) == row), arrived)
    low_ref[...] = placed[:HALF]
    high_ref[...] = placed[HALF:]


def add_kernel(first_ref, second_ref, third_ref, fourth_ref, early_ref, late_ref):
    total = first_ref[...] + second_ref[...] + (third_ref[...] + fourth_ref[...])
    early_ref[...] = total[:HALF]
    late_ref[...] = total[HALF:]


def remainder(x, by):
    return x - jnp.floor((x + 0.5) * (1.0 / by)) * by


def pack_kernel(each, position_ref, low_ref, high_ref, sums_ref, message_ref):
    size = each + ADDED
    total = message_ref.shape[0]
    grads = jnp.concatenate([low_ref[...], high_ref[...]], axis=0)
    sums = sums_ref[0]
    for part in range(1, sums_ref.shape[0]):
        sums += sums_ref[part]
    shape = (total, SIDE)
    row = iota(1, shape)
    added = jnp.floor((row + 0.5) * (1.0 / 32))
    rest = row - added * 32
    core = jnp.floor((rest + 0.5) * (1.0 / 16))
    peer = 2 * (rest - core * 16) + core
    pick = one_hot(remainder(iota(0, shape), size * SIDE // ADDED) == peer * size + each + added)
    message = select_rows(one_hot(wide(position_ref[...]) == iota(1, (total, PATCH))), grads)
    message_ref[...] = message + select_rows(pick, sums)


def unpack_kernel(each, message_ref, sums_ref):
    size = each + ADDED
    shape = (SIDE, message_ref.shape[0])
    row = iota(0, shape)
    peer = jnp.floor((row + 0.5) * (1.0 / ADDED))
    wanted = peer * size + each + (row - peer * ADDED)
    sums_ref[...] = select_rows(one_hot(remainder(iota(1, shape), size * SIDE // ADDED) == wanted), message_ref[...])


def unsort_kernel(each, slot_ref, message_ref, out_ref):
    slot = slot_ref[...]
    block = jnp.floor((slot + 0.5) * (1.0 / each))
    wanted = block * (each + ADDED) + (slot - block * each)
    total = message_ref.shape[0]
    pick = one_hot(wide(column(wanted), total) == iota(1, (PATCH, total)))
    out_ref[...] = select_rows(pick, message_ref[...])


def finish_kernel(core_ref, mine_ref, other_ref, din_ref, dout_ref):
    core = core_ref[0]
    for own, ref in ((core, mine_ref), (1 - core, other_ref)):
        for block in range(BLOCKS):
            for side in range(2):
                for added in range(ADDED):
                    got = ref[:, (2 * block + side) * ADDED + added, :]
                    rows = pl.ds(pl.multiple_of(side * SIDE + added * 32 + own * 16, 16), 16)
                    t, part = divmod(block, D // WIDTH)
                    lanes = slice(part * WIDTH, (part + 1) * WIDTH)
                    if t < 3:
                        rows = pl.ds(pl.multiple_of(part * WIDTH + side * SIDE + added * 32 + own * 16, 16), 16)
                        din_ref[t, rows] = got
                    else:
                        dout_ref[rows, lanes] = got


def cot_kernel(cot_ref, wout_ref, grad_ref):
    total = jnp.zeros((PATCH, WIDTH), F32)
    for part in range(D // WIDTH):
        total += mm3(split(cot_ref[part]), split(wout_ref[:, part * WIDTH : (part + 1) * WIDTH]), NT)
    grad_ref[...] = total


def head_mask(head):
    lanes = lax.broadcasted_iota(jnp.int32, (PATCH, WIDTH), 1)
    return (lanes // HEAD) == head


def scores_of(queries, key_rows, mask):
    qh, ql = split(queries)
    kh, kl = split(jnp.where(mask, key_rows, 0.0))
    keys = jnp.concatenate([kh, kl], axis=1)
    return mm(keys, jnp.concatenate([qh, qh], axis=1), NT) + mm(
        keys, jnp.concatenate([ql, ql], axis=1), NT
    )


def forward_kernel(x_ref, win_ref, wout_ref, bias_ref, qkv_ref, att_ref, lse_ref, out_ref, vt_ref):
    parts = [split(x_ref[part]) for part in range(D // WIDTH)]
    for t in range(3):
        total = jnp.zeros((PATCH, WIDTH), F32)
        for part in range(D // WIDTH):
            total += mm3(parts[part], split(win_ref[t, part * WIDTH : (part + 1) * WIDTH]))
        qkv_ref[t] = total
    vt_ref[...] = jnp.transpose(qkv_ref[2])
    bias = wide(bias_ref[...])

    def one(head, carry):
        mask = head_mask(head)
        scores = scores_of(qkv_ref[0] * (SCALE * LOG2E), qkv_ref[1], mask) + bias
        top = jnp.max(scores, axis=0, keepdims=True)
        weights = jnp.exp2(scores - top)
        total = jnp.sum(weights, axis=0, keepdims=True)
        rows = pl.ds(pl.multiple_of(head * HEAD, HEAD), HEAD)
        vh, vl = split(vt_ref[rows, :])
        wh, wl = split(weights)
        both = mm(jnp.concatenate([vh, vl], axis=0), wh)
        attended = both[:HEAD] + both[HEAD:] + mm(vh, wl)
        att_ref[rows, :] = attended / total
        lse_ref[pl.ds(head, 1), :] = top + jnp.log2(total)
        return carry

    lax.fori_loop(0, HERE, one, 0)
    attended = split(jnp.transpose(att_ref[...]))
    for part in range(D // WIDTH):
        out_ref[part] = mm3(attended, split(wout_ref[:, part * WIDTH : (part + 1) * WIDTH]))


def backward_kernel(qkv_ref, att_ref, lse_ref, grad_ref, bias_ref, dqkv_ref, kt_ref, gt_ref, dqt_ref):
    kt_ref[...] = jnp.transpose(qkv_ref[1])
    gt_ref[...] = jnp.transpose(grad_ref[...])
    bias = wide(bias_ref[...])
    dqkv_ref[1] = jnp.zeros((PATCH, WIDTH), F32)
    dqkv_ref[2] = jnp.zeros((PATCH, WIDTH), F32)

    def one(head, carry):
        mask = head_mask(head)
        rows = pl.ds(pl.multiple_of(head * HEAD, HEAD), HEAD)
        scores = scores_of(qkv_ref[0] * (SCALE * LOG2E), qkv_ref[1], mask) + bias
        probs = jnp.exp2(scores - lse_ref[pl.ds(head, 1), :])
        ph, plo = split(probs)
        grad_probs = scores_of(grad_ref[...], qkv_ref[2], mask)
        gh, gl = split(jnp.where(mask, grad_ref[...], 0.0))
        both = mm(ph, jnp.concatenate([gh, gl], axis=1))
        dqkv_ref[2] += both[:, :WIDTH] + both[:, WIDTH:] + mm(plo, gh)
        inner = jnp.sum(gt_ref[rows, :] * att_ref[rows, :], axis=0, keepdims=True)
        grad_scores = probs * (grad_probs - inner)
        sh, sl = split(grad_scores)
        qh, ql = split(jnp.where(mask, qkv_ref[0] * SCALE, 0.0))
        both = mm(sh, jnp.concatenate([qh, ql], axis=1))
        dqkv_ref[1] += both[:, :WIDTH] + both[:, WIDTH:] + mm(sl, qh)
        kh, kl = split(kt_ref[rows, :] * SCALE)
        both = mm(jnp.concatenate([kh, kl], axis=0), sh)
        dqt_ref[rows, :] = both[:HEAD] + both[HEAD:] + mm(kh, sl)
        return carry

    lax.fori_loop(0, HERE, one, 0)
    dqkv_ref[0] = jnp.transpose(dqt_ref[...])


def weights_kernel(core_ref, x_ref, dqkv_ref, att_ref, cot_ref, keep_ref, send_ref):
    second = core_ref[0] == 1

    def put(block, grads):
        top, bottom = grads[:SIDE], grads[SIDE:]
        keep_ref[block] = jnp.where(second, bottom, top)
        send_ref[block] = jnp.where(second, top, bottom)

    attended = split(att_ref[...])
    parts = [split(x_ref[part]) for part in range(D // WIDTH)]
    for t in range(3):
        grads = split(jnp.transpose(dqkv_ref[t]))
        for part in range(D // WIDTH):
            put(t * (D // WIDTH) + part, jnp.transpose(mm3(grads, parts[part])))
    for part in range(D // WIDTH):
        put(3 * (D // WIDTH) + part, mm3(attended, split(cot_ref[part])))


def rows_kernel(head_ref, dqkv_ref, win_ref, *out_refs):
    grads = [split(dqkv_ref[t]) for t in range(3)]
    for step, out_ref in enumerate(out_refs):
        part = lax.rem(head_ref[0] + step, D // WIDTH)
        rows = pl.ds(pl.multiple_of(part * WIDTH, WIDTH), WIDTH)
        total = jnp.zeros((PATCH, WIDTH), F32)
        for t in range(3):
            total += mm3(grads[t], split(win_ref[t, rows]), NT)
        out_ref[...] = total


def call(kernel, outs, *args, scratch=(), scalars=0, flops=10**9):
    size = sum(math.prod(a.shape) * 4 for a in (*args, *outs))
    return pl.pallas_call(
        kernel,
        out_shape=tuple(jax.ShapeDtypeStruct(o, F32) for o in [x.shape for x in outs]),
        in_specs=[pl.BlockSpec(memory_space=pltpu.SMEM)] * scalars
        + [pl.BlockSpec(memory_space=pltpu.VMEM)] * (len(args) - scalars),
        out_specs=tuple(pl.BlockSpec(memory_space=pltpu.VMEM) for _ in outs),
        scratch_shapes=[pltpu.VMEM(s, F32) for s in scratch],
        compiler_params=pltpu.CompilerParams(vmem_limit_bytes=40 * 2**20),
        cost_estimate=pl.CostEstimate(flops=flops, bytes_accessed=size, transcendentals=0),
    )(*args)


def of(*shape):
    return jax.ShapeDtypeStruct(shape, F32)


def swap(x, axis):
    return lax.all_to_all(x, axis, split_axis=0, concat_axis=0, tiled=True)


def spread_to(x, axis):
    peers = lax.axis_size(axis)
    return swap(jnp.broadcast_to(x[None], (peers,) + x.shape).reshape(-1, WIDTH), axis)


def shards(features, input_proj, output_proj, destination, real_points, cotangent):
    peers = lax.axis_size(CURVE)
    heads = lax.axis_size("head")
    each = PATCH // peers
    up = [(i, (i + 1) % peers) for i in range(peers)]
    down = [(j, i) for i, j in up]
    core = lax.axis_index("core").astype(jnp.int32).reshape(1)
    head = lax.axis_index("head").astype(jnp.int32).reshape(1)

    def to_patch(low, high):
        return jnp.concatenate([lax.ppermute(high, CURVE, up), low], axis=0)

    def exchange(message):
        rows = message.shape[0]
        return swap(message.reshape(rows, 1, WIDTH), CURVE).reshape(rows, WIDTH)

    message, slot = call(
        functools.partial(sort_kernel, each), [of(PATCH + peers, WIDTH), of(1, PATCH)],
        destination.reshape(1, PATCH), features,
    )
    arrived = exchange(message)
    cot = lax.all_gather(to_patch(cotangent[:HALF], cotangent[HALF:]), "head", axis=0)
    win = jnp.transpose(input_proj, (1, 0, 2))
    valid = to_patch(real_points[:HALF], real_points[HALF:])
    bias = jnp.broadcast_to(jnp.where(valid > 0, 0.0, -jnp.inf).astype(F32)[:, None], (PATCH, WIDTH))
    (grad_attended,) = call(cot_kernel, [of(PATCH, WIDTH)], cot, output_proj)
    low, high = call(functools.partial(place_kernel, each), [of(HALF, WIDTH)] * 2, arrived)
    (position,) = call(
        functools.partial(positions_kernel, each), [of(peers * (each + ADDED), WIDTH)], arrived
    )
    x = spread_to(to_patch(low, high), "head").reshape(D // WIDTH, PATCH, WIDTH)
    qkv, attended, lse, out = call(
        forward_kernel,
        [of(3, PATCH, WIDTH), of(WIDTH, PATCH), of(HERE, PATCH), of(D // WIDTH, PATCH, WIDTH)],
        x, win, output_proj, bias, scratch=[(WIDTH, PATCH)],
    )
    out = lax.psum_scatter(out, "head", scatter_dimension=0)
    branch_out = jnp.concatenate([out[HALF:], lax.ppermute(out[:HALF], CURVE, down)], axis=0)
    (dqkv,) = call(
        backward_kernel, [of(3, PATCH, WIDTH)], qkv, attended, lse, grad_attended, bias,
        scratch=[(WIDTH, PATCH)] * 3,
    )
    dx = call(rows_kernel, [of(PATCH, WIDTH)] * heads, head, dqkv, win, scalars=1)
    dx = [dx[0]] + [
        lax.ppermute(dx[s], "head", [(i, (i + s) % heads) for i in range(heads)]) for s in (2, 1, 3)
    ]
    keep, send = call(
        weights_kernel, [of(BLOCKS, SIDE, WIDTH)] * 2, core, x, dqkv, attended, cot, scalars=1
    )
    sums = keep + lax.ppermute(send, "core", [(0, 1), (1, 0)])
    sums = swap(sums.reshape(-1, WIDTH), PLANE).reshape(BLOCKS, SIDE, WIDTH)
    early, late = call(add_kernel, [of(HALF, WIDTH)] * 2, *dx)
    (message,) = call(
        functools.partial(pack_kernel, each), [of(peers * (each + ADDED), WIDTH)],
        position, late, lax.ppermute(early, CURVE, down), sums,
    )
    message = exchange(message)
    (sums,) = call(functools.partial(unpack_kernel, each), [of(SIDE, WIDTH)], message)
    (grad_features,) = call(functools.partial(unsort_kernel, each), [of(PATCH, WIDTH)], slot, message)
    sums = spread_to(sums, PLANE).reshape(BLOCKS, SIDE, WIDTH)
    grad_inproj, grad_outproj = call(
        finish_kernel, [of(3, D, WIDTH), of(WIDTH, D)],
        core, sums, lax.ppermute(sums, "core", [(0, 1), (1, 0)]), scalars=1,
    )
    return (branch_out, grad_features, jnp.transpose(grad_inproj, (1, 0, 2)), grad_outproj)


def solution(mesh):
    curve, head = mesh.devices.shape
    sizes = (curve // 32, 4, 4, 2)
    fine = jax.sharding.Mesh(mesh.devices.reshape(*sizes, head), CURVE + ("head",))
    return jax.shard_map(
        shards,
        mesh=fine,
        in_specs=(
            P(CURVE, "head"),
            P(None, None, "head"),
            P("head", None),
            P(CURVE),
            P(CURVE),
            P(CURVE, "head"),
        ),
        out_specs=(P(CURVE, "head"), P(CURVE, "head"), P(None, None, "head"), P("head", None)),
        check_vma=False,
    )
```

```python
import functools
import math

import jax
import jax.numpy as jnp
from jax import lax
from jax.experimental import pallas as pl
from jax.experimental.pallas import tpu as pltpu
from jax.sharding import PartitionSpec as P

D = 512
HEADS = 16
PATCH = 512
HALF = PATCH // 2
HEAD = D // HEADS
WIDTH = 128
HERE = WIDTH // HEAD
CURVE = ("far", "near", "x", "core")
PLANE = ("near", "x")
BLOCKS = 16
SIDE = WIDTH // 2
ADDED = 2
BF = jnp.bfloat16
F32 = jnp.float32
SCALE = 1.0 / math.sqrt(HEAD)
LOG2E = math.log2(math.e)

NN = (((1,), (0,)), ((), ()))
NT = (((1,), (1,)), ((), ()))


def mm(a, b, dims=NN):
    return lax.dot_general(a, b, dims, preferred_element_type=F32)


def split(x):
    high = x.astype(BF)
    return high, (x - high.astype(F32)).astype(BF)


def split3(x):
    high, rest = x.astype(BF), None
    rest = x - high.astype(F32)
    mid = rest.astype(BF)
    return high, mid, (rest - mid.astype(F32)).astype(BF)


def mm3(a, b, dims=NN):
    (ah, al), (bh, bl) = a, b
    return mm(ah, bh, dims) + (mm(ah, bl, dims) + mm(al, bh, dims))


def select_rows(pick, x):
    high, mid, low = split3(x)
    return mm(pick, high) + (mm(pick, mid) + mm(pick, low))


def column(row):
    return jnp.transpose(jnp.broadcast_to(row, (WIDTH, row.shape[1])))


def wide(col, width=PATCH):
    return jnp.concatenate([col] * (width // WIDTH), axis=1)


def iota(dim, shape=(PATCH, PATCH)):
    return lax.broadcasted_iota(jnp.int32, shape, dim).astype(F32)


def one_hot(condition):
    return jnp.where(condition, 1.0, 0.0).astype(BF)


def every(ref, first, step):
    return ref[pl.ds(first, ref.shape[0] // step, stride=step), :]


def sort_kernel(each, dest_ref, feat_ref, message_ref, index_ref):
    peers = PATCH // each
    dest = dest_ref[...]
    block = dest // PATCH
    local = (dest - block * PATCH).astype(F32)
    block = block.astype(F32)
    same = (wide(column(block)) == block) & (iota(0) < iota(1))
    rank = jnp.sum(jnp.where(same, 1.0, 0.0), axis=0, keepdims=True)
    index = rank * peers + block
    index_ref[...] = index
    rows = select_rows(one_hot(iota(0) == index), feat_ref[...])
    for turn in range(each):
        message_ref[pl.ds(turn, peers, stride=each + 1), :] = rows[turn * peers : (turn + 1) * peers]
    high, low = split(jnp.where(iota(1, (PATCH, WIDTH)) == column(rank), column(local), 0.0))
    mine = one_hot(iota(0, (peers, PATCH)) == block)
    message_ref[pl.ds(each, peers, stride=each + 1), :] = mm(mine, high) + mm(mine, low)


def place_kernel(each, message_ref, valid_ref, after_ref, low_ref, high_ref, position_ref, bias_ref):
    del after_ref
    turned = jnp.transpose(every(message_ref, each, each + 1))
    position = jnp.concatenate([turned[turn : turn + 1] for turn in range(each)], axis=1)
    position_ref[...] = position
    arrived = jnp.concatenate([every(message_ref, turn, each + 1) for turn in range(each)], axis=0)
    placed = select_rows(one_hot(iota(0) == position), arrived)
    low_ref[...] = placed[:HALF]
    high_ref[...] = placed[HALF:]
    bias_ref[...] = column(jnp.where(valid_ref[...] > 0, 0.0, -jnp.inf))


def add_kernel(parts_ref, early_ref, late_ref):
    total = parts_ref[0] + parts_ref[1] + (parts_ref[2] + parts_ref[3])
    early_ref[...] = total[:HALF]
    late_ref[...] = total[HALF:]


def pack_kernel(each, position_ref, low_ref, high_ref, sums_ref, message_ref):
    peers = PATCH // each
    size = each + ADDED
    grads = jnp.concatenate([low_ref[...], high_ref[...]], axis=0)
    rows = select_rows(one_hot(wide(column(position_ref[...])) == iota(1)), grads)
    for turn in range(each):
        message_ref[pl.ds(turn, peers, stride=size), :] = rows[turn * peers : (turn + 1) * peers]
    sums = sums_ref[0]
    for part in range(1, sums_ref.shape[0]):
        sums += sums_ref[part]
    near = SIDE // ADDED
    for turn in range(ADDED):
        rows = jnp.concatenate([sums[turn * near : (turn + 1) * near]] * (peers // near), axis=0)
        message_ref[pl.ds(each + turn, peers, stride=size), :] = rows


def unpack_kernel(each, message_ref, sums_ref):
    near = SIDE // ADDED
    for turn in range(ADDED):
        rows = every(message_ref, each + turn, each + ADDED)
        total = rows[:near]
        for far in range(1, rows.shape[0] // near):
            total += rows[far * near : (far + 1) * near]
        sums_ref[turn * near : (turn + 1) * near] = total


def unsort_kernel(each, index_ref, message_ref, out_ref):
    returned = jnp.concatenate([every(message_ref, turn, each + ADDED) for turn in range(each)], axis=0)
    out_ref[...] = select_rows(one_hot(wide(column(index_ref[...])) == iota(1)), returned)


def finish_kernel(core_ref, mine_ref, other_ref, din_ref, dout_ref, out_ref):
    core = core_ref[0]
    near = SIDE // ADDED
    for own, ref in ((core, mine_ref), (1 - core, other_ref)):
        for block in range(BLOCKS):
            t, part = divmod(block, D // WIDTH)
            for side in range(2):
                for turn in range(ADDED):
                    got = ref[:, turn * near + 2 * block + side, :]
                    first = side * SIDE + turn * near + own
                    if t < 3:
                        din_ref[t, pl.ds(part * WIDTH + first, BLOCKS, stride=2), :] = got
                    else:
                        out_ref[part, pl.ds(first, BLOCKS, stride=2), :] = got
    for part in range(D // WIDTH):
        dout_ref[:, part * WIDTH : (part + 1) * WIDTH] = out_ref[part]


def head_mask(head):
    lanes = lax.broadcasted_iota(jnp.int32, (PATCH, WIDTH), 1)
    return (lanes // HEAD) == head


def scores_of(queries, key_rows, mask):
    qh, ql = split(queries)
    kh, kl = split(jnp.where(mask, key_rows, 0.0))
    keys = jnp.concatenate([kh, kl], axis=1)
    return mm(keys, jnp.concatenate([qh, qh], axis=1), NT) + mm(
        keys, jnp.concatenate([ql, ql], axis=1), NT
    )


def forward_kernel(x_ref, win_ref, wout_ref, bias_ref, qkv_ref, att_ref, lse_ref, out_ref, vt_ref):
    parts = [split(x_ref[part]) for part in range(D // WIDTH)]
    for t in range(3):
        total = jnp.zeros((PATCH, WIDTH), F32)
        for part in range(D // WIDTH):
            total += mm3(parts[part], split(win_ref[t, part * WIDTH : (part + 1) * WIDTH]))
        qkv_ref[t] = total
    vt_ref[...] = jnp.transpose(qkv_ref[2])
    bias = wide(bias_ref[...])

    def one(head, carry):
        mask = head_mask(head)
        scores = scores_of(qkv_ref[0] * (SCALE * LOG2E), qkv_ref[1], mask) + bias
        top = jnp.max(scores, axis=0, keepdims=True)
        weights = jnp.exp2(scores - top)
        total = jnp.sum(weights, axis=0, keepdims=True)
        rows = pl.ds(pl.multiple_of(head * HEAD, HEAD), HEAD)
        vh, vl = split(vt_ref[rows, :])
        wh, wl = split(weights)
        both = mm(jnp.concatenate([vh, vl], axis=0), wh)
        attended = both[:HEAD] + both[HEAD:] + mm(vh, wl)
        att_ref[rows, :] = attended / total
        lse_ref[pl.ds(head, 1), :] = top + jnp.log2(total)
        return carry

    lax.fori_loop(0, HERE, one, 0)
    attended = split(jnp.transpose(att_ref[...]))
    for part in range(D // WIDTH):
        out_ref[part] = mm3(attended, split(wout_ref[:, part * WIDTH : (part + 1) * WIDTH]))


def backward_kernel(
    qkv_ref, att_ref, lse_ref, before_ref, cot_ref, wout_ref, bias_ref, dqkv_ref, kt_ref, gt_ref, dqt_ref, grad_ref
):
    for rows, ref, first in ((slice(0, HALF), before_ref, 0), (slice(HALF, PATCH), cot_ref, 0)):
        total = jnp.zeros((HALF, WIDTH), F32)
        for part in range(D // WIDTH):
            lanes = slice(part * WIDTH, (part + 1) * WIDTH)
            total += mm3(split(ref[part, first : first + HALF]), split(wout_ref[:, lanes]), NT)
        grad_ref[rows] = total
    kt_ref[...] = jnp.transpose(qkv_ref[1])
    gt_ref[...] = jnp.transpose(grad_ref[...])
    bias = wide(bias_ref[...])
    dqkv_ref[1] = jnp.zeros((PATCH, WIDTH), F32)
    dqkv_ref[2] = jnp.zeros((PATCH, WIDTH), F32)

    def one(head, carry):
        mask = head_mask(head)
        rows = pl.ds(pl.multiple_of(head * HEAD, HEAD), HEAD)
        scores = scores_of(qkv_ref[0] * (SCALE * LOG2E), qkv_ref[1], mask) + bias
        probs = jnp.exp2(scores - lse_ref[pl.ds(head, 1), :])
        ph, plo = split(probs)
        grad_probs = scores_of(grad_ref[...], qkv_ref[2], mask)
        gh, gl = split(jnp.where(mask, grad_ref[...], 0.0))
        both = mm(ph, jnp.concatenate([gh, gl], axis=1))
        dqkv_ref[2] += both[:, :WIDTH] + both[:, WIDTH:] + mm(plo, gh)
        inner = jnp.sum(gt_ref[rows, :] * att_ref[rows, :], axis=0, keepdims=True)
        grad_scores = probs * (grad_probs - inner)
        sh, sl = split(grad_scores)
        qh, ql = split(jnp.where(mask, qkv_ref[0] * SCALE, 0.0))
        both = mm(sh, jnp.concatenate([qh, ql], axis=1))
        dqkv_ref[1] += both[:, :WIDTH] + both[:, WIDTH:] + mm(sl, qh)
        kh, kl = split(kt_ref[rows, :] * SCALE)
        both = mm(jnp.concatenate([kh, kl], axis=0), sh)
        dqt_ref[rows, :] = both[:HEAD] + both[HEAD:] + mm(kh, sl)
        return carry

    lax.fori_loop(0, HERE, one, 0)
    dqkv_ref[0] = jnp.transpose(dqt_ref[...])


def weights_kernel(core_ref, x_ref, dqkv_ref, att_ref, before_ref, cot_ref, after_ref, keep_ref, send_ref):
    del after_ref
    second = core_ref[0] == 1

    def put(block, grads):
        top, bottom = grads[:SIDE], grads[SIDE:]
        keep_ref[block] = jnp.where(second, bottom, top)
        send_ref[block] = jnp.where(second, top, bottom)

    attended = split(att_ref[...])
    parts = [split(x_ref[part]) for part in range(D // WIDTH)]
    for t in range(3):
        grads = split(jnp.transpose(dqkv_ref[t]))
        for part in range(D // WIDTH):
            put(t * (D // WIDTH) + part, jnp.transpose(mm3(grads, parts[part])))
    for part in range(D // WIDTH):
        cot = jnp.concatenate([before_ref[part], cot_ref[part, :HALF]], axis=0)
        put(3 * (D // WIDTH) + part, mm3(attended, split(cot)))


def rows_kernel(dqkv_ref, win_ref, dx_ref, done_ref):
    done_ref[...] = jnp.zeros_like(done_ref)
    grads = [split(dqkv_ref[t]) for t in range(3)]
    for part in range(D // WIDTH):
        total = jnp.zeros((PATCH, WIDTH), F32)
        for t in range(3):
            total += mm3(grads[t], split(win_ref[t, part * WIDTH : (part + 1) * WIDTH]), NT)
        dx_ref[part] = total


def call(kernel, outs, *args, scratch=(), scalars=0, room=8, flops=10**9):
    size = sum(math.prod(a.shape) * 4 for a in (*args, *outs))
    return pl.pallas_call(
        kernel,
        out_shape=tuple(jax.ShapeDtypeStruct(o, F32) for o in [x.shape for x in outs]),
        in_specs=[pl.BlockSpec(memory_space=pltpu.SMEM)] * scalars
        + [pl.BlockSpec(memory_space=pltpu.VMEM)] * (len(args) - scalars),
        out_specs=tuple(pl.BlockSpec(memory_space=pltpu.VMEM) for _ in outs),
        scratch_shapes=[pltpu.VMEM(s, F32) for s in scratch],
        compiler_params=pltpu.CompilerParams(vmem_limit_bytes=room * 2**20),
        cost_estimate=pl.CostEstimate(flops=flops, bytes_accessed=size, transcendentals=0),
    )(*args)


def of(*shape):
    return jax.ShapeDtypeStruct(shape, F32)


def swap(x, axis):
    return lax.all_to_all(x, axis, split_axis=0, concat_axis=0, tiled=True)


def spread_to(x, axis):
    peers = lax.axis_size(axis)
    return swap(jnp.broadcast_to(x[None], (peers,) + x.shape).reshape(-1, WIDTH), axis)


def shards(features, input_proj, output_proj, destination, real_points, cotangent):
    peers = lax.axis_size(CURVE)
    each = PATCH // peers
    up = [(i, (i + 1) % peers) for i in range(peers)]
    down = [(j, i) for i, j in up]
    core = lax.axis_index("core").astype(jnp.int32).reshape(1)

    def to_patch(low, high):
        return jnp.concatenate([lax.ppermute(high, CURVE, up), low], axis=0)

    def exchange(message):
        rows = message.shape[0]
        return swap(message.reshape(rows, 1, WIDTH), CURVE).reshape(rows, WIDTH)

    cot = lax.all_gather(cotangent, "head", axis=0)
    message, index = call(
        functools.partial(sort_kernel, each), [of(PATCH + peers, WIDTH), of(1, PATCH)],
        destination.reshape(1, PATCH), features,
    )
    arrived = exchange(message)
    win = jnp.transpose(input_proj, (1, 0, 2))
    valid = to_patch(real_points[:HALF], real_points[HALF:]).reshape(1, PATCH)
    low, high, position, bias = call(
        functools.partial(place_kernel, each),
        [of(HALF, WIDTH), of(HALF, WIDTH), of(1, PATCH), of(PATCH, WIDTH)], arrived, valid, cot[0, :8],
    )
    x = spread_to(to_patch(low, high), "head").reshape(D // WIDTH, PATCH, WIDTH)
    qkv, attended, lse, out = call(
        forward_kernel,
        [of(3, PATCH, WIDTH), of(WIDTH, PATCH), of(HERE, PATCH), of(D // WIDTH, PATCH, WIDTH)],
        x, win, output_proj, bias, scratch=[(WIDTH, PATCH)], room=16,
    )
    out = lax.psum_scatter(out, "head", scatter_dimension=0)
    branch_out = jnp.concatenate([out[HALF:], lax.ppermute(out[:HALF], CURVE, down)], axis=0)
    before = lax.ppermute(cot[:, HALF:], CURVE, up)
    (dqkv,) = call(
        backward_kernel, [of(3, PATCH, WIDTH)], qkv, attended, lse, before, cot, output_proj, bias,
        scratch=[(WIDTH, PATCH)] * 3 + [(PATCH, WIDTH)], room=16,
    )
    dx, done = call(rows_kernel, [of(D // WIDTH, PATCH, WIDTH), of(8, WIDTH)], dqkv, win)
    dx = swap(dx.reshape(-1, WIDTH), "head").reshape(D // WIDTH, PATCH, WIDTH)
    early, late = call(add_kernel, [of(HALF, WIDTH)] * 2, dx)
    keep, send = call(
        weights_kernel, [of(BLOCKS, SIDE, WIDTH)] * 2, core, x, dqkv, attended, before, cot, done, scalars=1
    )
    sums = keep + lax.ppermute(send, "core", [(0, 1), (1, 0)])
    sums, early = lax.optimization_barrier((sums, early))
    sums = swap(sums.reshape(-1, WIDTH), PLANE).reshape(BLOCKS, SIDE, WIDTH)
    (message,) = call(
        functools.partial(pack_kernel, each), [of(peers * (each + ADDED), WIDTH)],
        position, late, lax.ppermute(early, CURVE, down), sums,
    )
    message = exchange(message)
    (sums,) = call(functools.partial(unpack_kernel, each), [of(SIDE, WIDTH)], message)
    (grad_features,) = call(functools.partial(unsort_kernel, each), [of(PATCH, WIDTH)], index, message)
    sums, branch_out = lax.optimization_barrier((sums, branch_out))
    sums = spread_to(sums, PLANE).reshape(BLOCKS, SIDE, WIDTH)
    sums, grad_features = lax.optimization_barrier((sums, grad_features))
    grad_inproj, grad_outproj = call(
        finish_kernel, [of(3, D, WIDTH), of(WIDTH, D)],
        core, sums, lax.ppermute(sums, "core", [(0, 1), (1, 0)]), scalars=1,
        scratch=[(D // WIDTH, WIDTH, WIDTH)],
    )
    return (branch_out, grad_features, jnp.transpose(grad_inproj, (1, 0, 2)), grad_outproj)


def solution(mesh):
    curve, head = mesh.devices.shape
    sizes = (curve // 32, 4, 4, 2)
    fine = jax.sharding.Mesh(mesh.devices.reshape(*sizes, head), CURVE + ("head",))
    return jax.shard_map(
        shards,
        mesh=fine,
        in_specs=(
            P(CURVE, "head"),
            P(None, None, "head"),
            P("head", None),
            P(CURVE),
            P(CURVE),
            P(CURVE, "head"),
        ),
        out_specs=(P(CURVE, "head"), P(CURVE, "head"), P(None, None, "head"), P("head", None)),
        check_vma=False,
    )
```

```python
import functools
import math

import jax
import jax.numpy as jnp
from jax import lax
from jax.experimental import pallas as pl
from jax.experimental.pallas import tpu as pltpu
from jax.sharding import PartitionSpec as P

D = 512
HEADS = 16
PATCH = 512
HALF = PATCH // 2
HEAD = D // HEADS
WIDTH = 128
HERE = WIDTH // HEAD
CURVE = ("far", "near", "x", "core")
PLANE = ("near", "x")
BLOCKS = 16
SIDE = WIDTH // 2
ADDED = 2
BF = jnp.bfloat16
F32 = jnp.float32
SCALE = 1.0 / math.sqrt(HEAD)
LOG2E = math.log2(math.e)

NN = (((1,), (0,)), ((), ()))
NT = (((1,), (1,)), ((), ()))


def mm(a, b, dims=NN):
    return lax.dot_general(a, b, dims, preferred_element_type=F32)


def split(x):
    high = x.astype(BF)
    return high, (x - high.astype(F32)).astype(BF)


def split3(x):
    high, rest = x.astype(BF), None
    rest = x - high.astype(F32)
    mid = rest.astype(BF)
    return high, mid, (rest - mid.astype(F32)).astype(BF)


def mm3(a, b, dims=NN):
    (ah, al), (bh, bl) = a, b
    (left,), (right,) = dims[0]
    return mm(jnp.concatenate([ah, al, ah], axis=left), jnp.concatenate([bh, bh, bl], axis=right), dims)


def select_rows(pick, x):
    high, mid, low = split3(x)
    return mm(pick, high) + (mm(pick, mid) + mm(pick, low))


def column(row):
    return jnp.transpose(jnp.broadcast_to(row, (WIDTH, row.shape[1])))


def wide(col, width=PATCH):
    return jnp.concatenate([col] * (width // WIDTH), axis=1)


def iota(dim, shape=(PATCH, PATCH)):
    return lax.broadcasted_iota(jnp.int32, shape, dim).astype(F32)


def one_hot(condition):
    return jnp.where(condition, 1.0, 0.0).astype(BF)


def every(ref, first, step):
    return ref[pl.ds(first, ref.shape[0] // step, stride=step), :]


def sort_kernel(each, dest_ref, feat_ref, message_ref, index_ref):
    peers = PATCH // each
    dest = dest_ref[...]
    block = dest // PATCH
    local = (dest - block * PATCH).astype(F32)
    block = block.astype(F32)
    same = (wide(column(block)) == block) & (iota(0) < iota(1))
    rank = jnp.sum(jnp.where(same, 1.0, 0.0), axis=0, keepdims=True)
    index = rank * peers + block
    index_ref[...] = index
    rows = select_rows(one_hot(iota(0) == index), feat_ref[...])
    for turn in range(each):
        message_ref[pl.ds(turn, peers, stride=each + 1), :] = rows[turn * peers : (turn + 1) * peers]
    high, low = split(jnp.where(iota(1, (PATCH, WIDTH)) == column(rank), column(local), 0.0))
    mine = one_hot(iota(0, (peers, PATCH)) == block)
    message_ref[pl.ds(each, peers, stride=each + 1), :] = mm(mine, high) + mm(mine, low)


def place_kernel(each, message_ref, valid_ref, after_ref, low_ref, high_ref, position_ref, bias_ref):
    del after_ref
    turned = jnp.transpose(every(message_ref, each, each + 1))
    position = jnp.concatenate([turned[turn : turn + 1] for turn in range(each)], axis=1)
    position_ref[...] = position
    arrived = jnp.concatenate([every(message_ref, turn, each + 1) for turn in range(each)], axis=0)
    placed = select_rows(one_hot(iota(0) == position), arrived)
    low_ref[...] = placed[:HALF]
    high_ref[...] = placed[HALF:]
    bias_ref[...] = column(jnp.where(valid_ref[...] > 0, 0.0, -jnp.inf))


def add_kernel(parts_ref, early_ref, late_ref):
    total = parts_ref[0] + parts_ref[1] + (parts_ref[2] + parts_ref[3])
    early_ref[...] = total[:HALF]
    late_ref[...] = total[HALF:]


def pack_kernel(each, position_ref, low_ref, high_ref, sums_ref, message_ref):
    peers = PATCH // each
    size = each + ADDED
    grads = jnp.concatenate([low_ref[...], high_ref[...]], axis=0)
    rows = select_rows(one_hot(wide(column(position_ref[...])) == iota(1)), grads)
    for turn in range(each):
        message_ref[pl.ds(turn, peers, stride=size), :] = rows[turn * peers : (turn + 1) * peers]
    sums = sums_ref[0]
    for part in range(1, sums_ref.shape[0]):
        sums += sums_ref[part]
    near = SIDE // ADDED
    for turn in range(ADDED):
        rows = jnp.concatenate([sums[turn * near : (turn + 1) * near]] * (peers // near), axis=0)
        message_ref[pl.ds(each + turn, peers, stride=size), :] = rows


def unpack_kernel(each, message_ref, out_hbm, sums_ref, sems):
    near = SIDE // ADDED
    for turn in range(ADDED):
        rows = every(message_ref, each + turn, each + ADDED)
        total = rows[:near]
        for far in range(1, rows.shape[0] // near):
            total += rows[far * near : (far + 1) * near]
        sums_ref[turn * near : (turn + 1) * near] = total
    copies = [pltpu.make_async_copy(sums_ref, out_hbm.at[i], sems.at[i]) for i in range(BLOCKS)]
    for copy in copies:
        copy.start()
    for copy in copies:
        copy.wait()


def unsort_kernel(each, index_ref, message_ref, out_ref):
    returned = jnp.concatenate([every(message_ref, turn, each + ADDED) for turn in range(each)], axis=0)
    out_ref[...] = select_rows(one_hot(wide(column(index_ref[...])) == iota(1)), returned)


def finish_kernel(core_ref, mine_ref, other_ref, din_ref, dout_ref, out_ref):
    core = core_ref[0]
    near = SIDE // ADDED
    for own, ref in ((core, mine_ref), (1 - core, other_ref)):
        for block in range(BLOCKS):
            t, part = divmod(block, D // WIDTH)
            for side in range(2):
                for turn in range(ADDED):
                    got = ref[:, turn * near + 2 * block + side, :]
                    first = side * SIDE + turn * near + own
                    if t < 3:
                        din_ref[t, pl.ds(part * WIDTH + first, BLOCKS, stride=2), :] = got
                    else:
                        out_ref[part, pl.ds(first, BLOCKS, stride=2), :] = got
    for part in range(D // WIDTH):
        dout_ref[:, part * WIDTH : (part + 1) * WIDTH] = out_ref[part]


def head_mask(head):
    lanes = lax.broadcasted_iota(jnp.int32, (PATCH, WIDTH), 1)
    return (lanes // HEAD) == head


def turned(x, order):
    high, low = split(x)
    parts = {"h": high.astype(F32), "l": low.astype(F32)}
    return [parts[o] if not i else pltpu.roll(parts[o], i * HEAD, 1) for i, o in enumerate(order)]


def of_head(refs, head):
    lanes = lax.broadcasted_iota(jnp.int32, (PATCH, WIDTH), 1)
    turn = (lanes // HEAD - head) & (HERE - 1)
    x = refs[0]
    for i in range(1, HERE):
        x = jnp.where(turn == i, refs[i], x)
    return x.astype(BF)


def keep(ref, parts):
    for i, part in enumerate(parts):
        ref[i] = part


def forward_kernel(x_ref, win_ref, bias_ref, qkv_ref, att_ref, lse_ref, vt_ref, q_ref, k_ref):
    x = jnp.concatenate([x_ref[part] for part in range(D // WIDTH)], axis=1)
    win = jnp.concatenate([win_ref[t] for t in range(3)], axis=1)
    qkv = mm3(split(x), split(win))
    for t in range(3):
        qkv_ref[t] = qkv[:, t * WIDTH : (t + 1) * WIDTH]
    vt_ref[...] = jnp.transpose(qkv_ref[2])
    keep(q_ref, turned(qkv_ref[0] * (SCALE * LOG2E), "hhll"))
    keep(k_ref, turned(qkv_ref[1], "hlhl"))
    bias = wide(bias_ref[...])

    def one(head, carry):
        scores = mm(of_head(k_ref, head), of_head(q_ref, head), NT) + bias
        top = jnp.max(scores, axis=0, keepdims=True)
        weights = jnp.exp2(scores - top)
        total = jnp.sum(weights, axis=0, keepdims=True)
        rows = pl.ds(pl.multiple_of(head * HEAD, HEAD), HEAD)
        vh, vl = split(vt_ref[rows, :])
        wh, wl = split(weights)
        both = mm(jnp.concatenate([vh, vl], axis=0), wh)
        attended = both[:HEAD] + both[HEAD:] + mm(vh, wl)
        att_ref[rows, :] = attended / total
        lse_ref[pl.ds(head, 1), :] = top + jnp.log2(total)
        return carry

    lax.fori_loop(0, HERE, one, 0, unroll=True)


def output_kernel(att_ref, wout_ref, after_ref, out_ref):
    del after_ref
    out = mm3(split(jnp.transpose(att_ref[...])), split(wout_ref[...]))
    for part in range(D // WIDTH):
        out_ref[part] = out[:, part * WIDTH : (part + 1) * WIDTH]


def backward_kernel(
    qkv_ref, att_ref, lse_ref, before_ref, cot_ref, wout_ref, bias_ref,
    dqkv_ref, kt_ref, gt_ref, dqt_ref, grad_ref, q_ref, k_ref, v_ref, g_ref,
):
    wout = split(wout_ref[...])
    for rows, ref in ((slice(0, HALF), before_ref), (slice(HALF, PATCH), cot_ref)):
        cot = jnp.concatenate([ref[part, :HALF] for part in range(D // WIDTH)], axis=1)
        grad_ref[rows] = mm3(split(cot), wout, NT)
    kt_ref[...] = jnp.transpose(qkv_ref[1])
    gt_ref[...] = jnp.transpose(grad_ref[...])
    keep(q_ref, turned(qkv_ref[0] * (SCALE * LOG2E), "hhll"))
    keep(k_ref, turned(qkv_ref[1], "hlhl"))
    keep(g_ref, turned(grad_ref[...], "hhll"))
    keep(v_ref, turned(qkv_ref[2], "hlhl"))
    bias = wide(bias_ref[...])
    dqkv_ref[1] = jnp.zeros((PATCH, WIDTH), F32)
    dqkv_ref[2] = jnp.zeros((PATCH, WIDTH), F32)

    def one(head, carry):
        mask = head_mask(head)
        rows = pl.ds(pl.multiple_of(head * HEAD, HEAD), HEAD)
        scores = mm(of_head(k_ref, head), of_head(q_ref, head), NT) + bias
        probs = jnp.exp2(scores - lse_ref[pl.ds(head, 1), :])
        ph, plo = split(probs)
        grad_probs = mm(of_head(v_ref, head), of_head(g_ref, head), NT)
        gh, gl = split(jnp.where(mask, grad_ref[...], 0.0))
        both = mm(ph, jnp.concatenate([gh, gl], axis=1))
        dqkv_ref[2] += both[:, :WIDTH] + both[:, WIDTH:] + mm(plo, gh)
        inner = jnp.sum(gt_ref[rows, :] * att_ref[rows, :], axis=0, keepdims=True)
        grad_scores = probs * (grad_probs - inner)
        sh, sl = split(grad_scores)
        qh, ql = split(jnp.where(mask, qkv_ref[0] * SCALE, 0.0))
        both = mm(sh, jnp.concatenate([qh, ql], axis=1))
        dqkv_ref[1] += both[:, :WIDTH] + both[:, WIDTH:] + mm(sl, qh)
        kh, kl = split(kt_ref[rows, :] * SCALE)
        both = mm(jnp.concatenate([kh, kl], axis=0), sh)
        dqt_ref[rows, :] = both[:HEAD] + both[HEAD:] + mm(kh, sl)
        return carry

    lax.fori_loop(0, HERE, one, 0, unroll=True)
    dqkv_ref[0] = jnp.transpose(dqt_ref[...])


def weights_kernel(core_ref, x_ref, dqkv_ref, att_ref, before_ref, cot_ref, after_ref, keep_ref, send_ref):
    del after_ref
    second = core_ref[0] == 1

    def put(block, grads):
        top, bottom = grads[:SIDE], grads[SIDE:]
        keep_ref[block] = jnp.where(second, bottom, top)
        send_ref[block] = jnp.where(second, top, bottom)

    x = split(jnp.concatenate([x_ref[part] for part in range(D // WIDTH)], axis=1))
    for t in range(3):
        grads = jnp.transpose(mm3(split(jnp.transpose(dqkv_ref[t])), x))
        for part in range(D // WIDTH):
            put(t * (D // WIDTH) + part, grads[part * WIDTH : (part + 1) * WIDTH])
    cot = [jnp.concatenate([ref[part, :HALF] for part in range(D // WIDTH)], axis=1) for ref in (before_ref, cot_ref)]
    grads = mm3(split(att_ref[...]), split(jnp.concatenate(cot, axis=0)))
    for part in range(D // WIDTH):
        put(3 * (D // WIDTH) + part, grads[:, part * WIDTH : (part + 1) * WIDTH])


def rows_kernel(dqkv_ref, win_ref, dx_ref, done_ref):
    done_ref[...] = jnp.zeros_like(done_ref)
    grads = split(jnp.concatenate([dqkv_ref[t] for t in range(3)], axis=1))
    for part in range(D // WIDTH):
        rows = slice(part * WIDTH, (part + 1) * WIDTH)
        win = jnp.concatenate([win_ref[t, rows] for t in range(3)], axis=1)
        dx_ref[part] = mm3(grads, split(win), NT)


def call(kernel, outs, *args, scratch=(), sems=(), scalars=0, sent=0, room=8, flops=10**9):
    size = sum(math.prod(a.shape) * 4 for a in (*args, *outs))
    vmem = pl.BlockSpec(memory_space=pltpu.VMEM)
    hbm = pl.BlockSpec(memory_space=pltpu.HBM)
    return pl.pallas_call(
        kernel,
        out_shape=tuple(jax.ShapeDtypeStruct(o, F32) for o in [x.shape for x in outs]),
        in_specs=[pl.BlockSpec(memory_space=pltpu.SMEM)] * scalars
        + [vmem] * (len(args) - scalars),
        out_specs=tuple([hbm] * sent + [vmem] * (len(outs) - sent)),
        scratch_shapes=[pltpu.VMEM(x, F32) if isinstance(x, tuple) else x for x in scratch]
        + [pltpu.SemaphoreType.DMA(n) for n in sems],
        compiler_params=pltpu.CompilerParams(vmem_limit_bytes=room * 2**20),
        cost_estimate=pl.CostEstimate(flops=flops, bytes_accessed=size, transcendentals=0),
    )(*args)


def of(*shape):
    return jax.ShapeDtypeStruct(shape, F32)


def swap(x, axis):
    return lax.all_to_all(x, axis, split_axis=0, concat_axis=0, tiled=True)


def shards(features, input_proj, output_proj, destination, real_points, cotangent):
    peers = lax.axis_size(CURVE)
    each = PATCH // peers
    up = [(i, (i + 1) % peers) for i in range(peers)]
    down = [(j, i) for i, j in up]
    core = lax.axis_index("core").astype(jnp.int32).reshape(1)

    def exchange(message):
        rows = message.shape[0]
        return swap(message.reshape(rows, 1, WIDTH), CURVE).reshape(rows, WIDTH)

    cot = lax.all_gather(cotangent, "head", axis=0)
    message, index = call(
        functools.partial(sort_kernel, each), [of(PATCH + peers, WIDTH), of(1, PATCH)],
        destination.reshape(1, PATCH), features,
    )
    arrived = exchange(message)
    win = jnp.transpose(input_proj, (1, 0, 2))
    valid = jnp.concatenate([lax.ppermute(real_points[HALF:], CURVE, up), real_points[:HALF]], axis=0)
    valid = valid.reshape(1, PATCH)
    low, high, position, bias = call(
        functools.partial(place_kernel, each),
        [of(HALF, WIDTH), of(HALF, WIDTH), of(1, PATCH), of(PATCH, WIDTH)], arrived, valid, cot[0, :8],
    )
    x = jnp.concatenate([lax.ppermute(high, CURVE, up), low], axis=0)
    x = jnp.broadcast_to(x[None], (D // WIDTH, PATCH, WIDTH))
    x = swap(x.reshape(-1, WIDTH), "head").reshape(D // WIDTH, PATCH, WIDTH)
    qkv, attended, lse = call(
        forward_kernel,
        [of(3, PATCH, WIDTH), of(WIDTH, PATCH), of(HERE, PATCH)],
        x, win, bias, scratch=[(WIDTH, PATCH)] + [(HERE, PATCH, WIDTH)] * 2, room=24,
    )
    before = lax.ppermute(cot[:, HALF:], CURVE, up)
    (dqkv,) = call(
        backward_kernel, [of(3, PATCH, WIDTH)], qkv, attended, lse, before, cot, output_proj, bias,
        scratch=[(WIDTH, PATCH)] * 3 + [(PATCH, WIDTH)] + [(HERE, PATCH, WIDTH)] * 4, room=24,
    )
    dx, done = call(
        rows_kernel, [of(D // WIDTH, PATCH, WIDTH), of(8, WIDTH)], dqkv, win
    )
    dx = swap(dx.reshape(-1, WIDTH), "head").reshape(D // WIDTH, PATCH, WIDTH)
    dx_early, dx_late = call(add_kernel, [of(HALF, WIDTH)] * 2, dx)
    keep, send = call(
        weights_kernel, [of(BLOCKS, SIDE, WIDTH)] * 2, core, x, dqkv, attended, before, cot, done, scalars=1
    )
    (out,) = call(output_kernel, [of(D // WIDTH, PATCH, WIDTH)], attended, output_proj, done)
    out = lax.psum_scatter(out, "head", scatter_dimension=0)
    branch_out = jnp.concatenate([out[HALF:], lax.ppermute(out[:HALF], CURVE, down)], axis=0)
    sums = keep + lax.ppermute(send, "core", [(0, 1), (1, 0)])
    sums, dx_early = lax.optimization_barrier((sums, dx_early))
    sums = swap(sums.reshape(-1, WIDTH), PLANE).reshape(BLOCKS, SIDE, WIDTH)
    (message,) = call(
        functools.partial(pack_kernel, each), [of(peers * (each + ADDED), WIDTH)],
        position, dx_late, lax.ppermute(dx_early, CURVE, down), sums,
    )
    message = exchange(message)
    (sums,) = call(
        functools.partial(unpack_kernel, each), [of(BLOCKS, SIDE, WIDTH)], message,
        sent=1, scratch=[(SIDE, WIDTH)], sems=[(BLOCKS,)],
    )
    sums, branch_out = lax.optimization_barrier((sums, branch_out))
    sums = swap(sums.reshape(-1, WIDTH), PLANE).reshape(BLOCKS, SIDE, WIDTH)
    sums, message = lax.optimization_barrier((sums, message))
    (grad_features,) = call(functools.partial(unsort_kernel, each), [of(PATCH, WIDTH)], index, message)
    grad_inproj, grad_outproj = call(
        finish_kernel, [of(3, D, WIDTH), of(WIDTH, D)],
        core, sums, lax.ppermute(sums, "core", [(0, 1), (1, 0)]), scalars=1,
        scratch=[(D // WIDTH, WIDTH, WIDTH)],
    )
    return (branch_out, grad_features, jnp.transpose(grad_inproj, (1, 0, 2)), grad_outproj)


def solution(mesh):
    curve, head = mesh.devices.shape
    sizes = (curve // 32, 4, 4, 2)
    fine = jax.sharding.Mesh(mesh.devices.reshape(*sizes, head), CURVE + ("head",))
    return jax.shard_map(
        shards,
        mesh=fine,
        in_specs=(
            P(CURVE, "head"),
            P(None, None, "head"),
            P("head", None),
            P(CURVE),
            P(CURVE),
            P(CURVE, "head"),
        ),
        out_specs=(P(CURVE, "head"), P(CURVE, "head"), P(None, None, "head"), P("head", None)),
        check_vma=False,
    )
```

```python
import functools
import math

import jax
import jax.numpy as jnp
from jax import lax
from jax.experimental import pallas as pl
from jax.experimental.pallas import tpu as pltpu
from jax.sharding import PartitionSpec as P

D = 512
HEADS = 16
PATCH = 512
HALF = PATCH // 2
HEAD = D // HEADS
WIDTH = 128
HERE = WIDTH // HEAD
CURVE = ("far", "near", "x", "core")
PLANE = ("near", "x")
BLOCKS = 16
SIDE = WIDTH // 2
ADDED = 2
BF = jnp.bfloat16
F32 = jnp.float32
SCALE = 1.0 / math.sqrt(HEAD)
LOG2E = math.log2(math.e)

NN = (((1,), (0,)), ((), ()))
NT = (((1,), (1,)), ((), ()))


def mm(a, b, dims=NN):
    return lax.dot_general(a, b, dims, preferred_element_type=F32)


def split(x):
    high = x.astype(BF)
    return high, (x - high.astype(F32)).astype(BF)


def split3(x):
    high, rest = x.astype(BF), None
    rest = x - high.astype(F32)
    mid = rest.astype(BF)
    return high, mid, (rest - mid.astype(F32)).astype(BF)


def mm3(a, b, dims=NN):
    (ah, al), (bh, bl) = a, b
    (left,), (right,) = dims[0]
    return mm(jnp.concatenate([ah, al, ah], axis=left), jnp.concatenate([bh, bh, bl], axis=right), dims)


def select_rows(pick, x):
    high, mid, low = split3(x)
    return mm(pick, high) + (mm(pick, mid) + mm(pick, low))


def column(row):
    return jnp.transpose(jnp.broadcast_to(row, (WIDTH, row.shape[1])))


def wide(col, width=PATCH):
    return jnp.concatenate([col] * (width // WIDTH), axis=1)


def iota(dim, shape=(PATCH, PATCH)):
    return lax.broadcasted_iota(jnp.int32, shape, dim).astype(F32)


def one_hot(condition):
    return jnp.where(condition, 1.0, 0.0).astype(BF)


def every(ref, first, step):
    return ref[pl.ds(first, ref.shape[0] // step, stride=step), :]


def sort_kernel(each, dest_ref, feat_ref, message_ref, index_ref):
    peers = PATCH // each
    dest = dest_ref[...]
    block = dest // PATCH
    local = (dest - block * PATCH).astype(F32)
    block = block.astype(F32)
    same = (wide(column(block)) == block) & (iota(0) < iota(1))
    rank = jnp.sum(jnp.where(same, 1.0, 0.0), axis=0, keepdims=True)
    index = rank * peers + block
    index_ref[...] = index
    rows = select_rows(one_hot(iota(0) == index), feat_ref[...])
    for turn in range(each):
        message_ref[pl.ds(turn, peers, stride=each + 1), :] = rows[turn * peers : (turn + 1) * peers]
    high, low = split(jnp.where(iota(1, (PATCH, WIDTH)) == column(rank), column(local), 0.0))
    mine = one_hot(iota(0, (peers, PATCH)) == block)
    message_ref[pl.ds(each, peers, stride=each + 1), :] = mm(mine, high) + mm(mine, low)


def place_kernel(each, after1_ref, after2_ref, after3_ref, message_ref, valid_ref, low_ref, high_ref, position_ref, bias_ref):
    del after1_ref, after2_ref, after3_ref
    turned = jnp.transpose(every(message_ref, each, each + 1))
    position = jnp.concatenate([turned[turn : turn + 1] for turn in range(each)], axis=1)
    position_ref[...] = position
    arrived = jnp.concatenate([every(message_ref, turn, each + 1) for turn in range(each)], axis=0)
    placed = select_rows(one_hot(iota(0) == position), arrived)
    low_ref[...] = placed[:HALF]
    high_ref[...] = placed[HALF:]
    bias_ref[...] = column(jnp.where(valid_ref[...] > 0, 0.0, -jnp.inf))


def add_kernel(parts_ref, early_ref, late_ref):
    total = parts_ref[0] + parts_ref[1] + (parts_ref[2] + parts_ref[3])
    early_ref[...] = total[:HALF]
    late_ref[...] = total[HALF:]


def pack_kernel(each, position_ref, low_ref, high_ref, sums_ref, message_ref):
    peers = PATCH // each
    size = each + ADDED
    grads = jnp.concatenate([low_ref[...], high_ref[...]], axis=0)
    rows = select_rows(one_hot(wide(column(position_ref[...])) == iota(1)), grads)
    for turn in range(each):
        message_ref[pl.ds(turn, peers, stride=size), :] = rows[turn * peers : (turn + 1) * peers]
    sums = sums_ref[0]
    for part in range(1, sums_ref.shape[0]):
        sums += sums_ref[part]
    near = SIDE // ADDED
    for turn in range(ADDED):
        rows = jnp.concatenate([sums[turn * near : (turn + 1) * near]] * (peers // near), axis=0)
        message_ref[pl.ds(each + turn, peers, stride=size), :] = rows


def unpack_kernel(each, message_ref, out_hbm, sums_ref, sems):
    near = SIDE // ADDED
    for turn in range(ADDED):
        rows = every(message_ref, each + turn, each + ADDED)
        total = rows[:near]
        for far in range(1, rows.shape[0] // near):
            total += rows[far * near : (far + 1) * near]
        sums_ref[turn * near : (turn + 1) * near] = total
    copies = [pltpu.make_async_copy(sums_ref, out_hbm.at[i], sems.at[i]) for i in range(BLOCKS)]
    for copy in copies:
        copy.start()
    for copy in copies:
        copy.wait()


def unsort_kernel(each, index_ref, message_ref, out_ref):
    returned = jnp.concatenate([every(message_ref, turn, each + ADDED) for turn in range(each)], axis=0)
    out_ref[...] = select_rows(one_hot(wide(column(index_ref[...])) == iota(1)), returned)


def finish_kernel(core_ref, mine_ref, other_ref, din_ref, dout_ref, out_ref):
    core = core_ref[0]
    near = SIDE // ADDED
    for own, ref in ((core, mine_ref), (1 - core, other_ref)):
        for block in range(BLOCKS):
            t, part = divmod(block, D // WIDTH)
            for side in range(2):
                for turn in range(ADDED):
                    got = ref[:, turn * near + 2 * block + side, :]
                    first = side * SIDE + turn * near + own
                    if t < 3:
                        din_ref[t, pl.ds(part * WIDTH + first, BLOCKS, stride=2), :] = got
                    else:
                        out_ref[part, pl.ds(first, BLOCKS, stride=2), :] = got
    for part in range(D // WIDTH):
        dout_ref[:, part * WIDTH : (part + 1) * WIDTH] = out_ref[part]


def head_mask(head):
    lanes = lax.broadcasted_iota(jnp.int32, (PATCH, WIDTH), 1)
    return (lanes // HEAD) == head


def turned(x, order):
    high, low = split(x)
    parts = {"h": high.astype(F32), "l": low.astype(F32)}
    return [parts[o] if not i else pltpu.roll(parts[o], i * HEAD, 1) for i, o in enumerate(order)]


def of_head(refs, head):
    lanes = lax.broadcasted_iota(jnp.int32, (PATCH, WIDTH), 1)
    turn = (lanes // HEAD - head) & (HERE - 1)
    x = refs[0]
    for i in range(1, HERE):
        x = jnp.where(turn == i, refs[i], x)
    return x.astype(BF)


def keep(ref, parts):
    for i, part in enumerate(parts):
        ref[i] = part


def forward_kernel(x_ref, win_ref, bias_ref, qkv_ref, att_ref, lse_ref, vt_ref, q_ref, k_ref):
    x = jnp.concatenate([x_ref[part] for part in range(D // WIDTH)], axis=1)
    win = jnp.concatenate([win_ref[t] for t in range(3)], axis=1)
    qkv = mm3(split(x), split(win))
    for t in range(3):
        qkv_ref[t] = qkv[:, t * WIDTH : (t + 1) * WIDTH]
    vt_ref[...] = jnp.transpose(qkv_ref[2])
    keep(q_ref, turned(qkv_ref[0] * (SCALE * LOG2E), "hhll"))
    keep(k_ref, turned(qkv_ref[1], "hlhl"))
    bias = wide(bias_ref[...])

    def one(head, carry):
        scores = mm(of_head(k_ref, head), of_head(q_ref, head), NT) + bias
        top = jnp.max(scores, axis=0, keepdims=True)
        weights = jnp.exp2(scores - top)
        total = jnp.sum(weights, axis=0, keepdims=True)
        rows = pl.ds(pl.multiple_of(head * HEAD, HEAD), HEAD)
        vh, vl = split(vt_ref[rows, :])
        wh, wl = split(weights)
        both = mm(jnp.concatenate([vh, vl], axis=0), wh)
        attended = both[:HEAD] + both[HEAD:] + mm(vh, wl)
        att_ref[rows, :] = attended / total
        lse_ref[pl.ds(head, 1), :] = top + jnp.log2(total)
        return carry

    lax.fori_loop(0, HERE, one, 0, unroll=True)


def along(step):
    part = lax.rem(step, D // WIDTH)
    return part, pl.ds(pl.multiple_of(part * WIDTH, WIDTH), WIDTH)


def output_kernel(head_ref, att_ref, wout_ref, after_ref, *out_refs):
    del after_ref
    attended = split(jnp.transpose(att_ref[...]))
    for step, out_ref in enumerate(out_refs):
        out_ref[...] = mm3(attended, split(wout_ref[:, along(head_ref[0] + step)[1]]))


def sum_kernel(first_ref, second_ref, third_ref, fourth_ref, early_ref, late_ref):
    total = first_ref[...] + second_ref[...] + (third_ref[...] + fourth_ref[...])
    early_ref[...] = total[:HALF]
    late_ref[...] = total[HALF:]


def backward_kernel(
    head_ref, qkv_ref, att_ref, lse_ref, before_ref, cot_ref, cot1_ref, cot2_ref, cot3_ref, wout_ref, bias_ref,
    dqkv_ref, kt_ref, gt_ref, dqt_ref, grad_ref, q_ref, k_ref, v_ref, g_ref,
):
    cots = [cot_ref, cot1_ref, cot2_ref, cot3_ref]
    cots = [jnp.concatenate([before_ref[s], ref[:HALF]], axis=0) for s, ref in enumerate(cots)]
    wout = [wout_ref[:, along(head_ref[0] + (D // WIDTH - s))[1]] for s in range(D // WIDTH)]
    grad_ref[...] = mm3(split(jnp.concatenate(cots, axis=1)), split(jnp.concatenate(wout, axis=1)), NT)
    kt_ref[...] = jnp.transpose(qkv_ref[1])
    gt_ref[...] = jnp.transpose(grad_ref[...])
    keep(q_ref, turned(qkv_ref[0] * (SCALE * LOG2E), "hhll"))
    keep(k_ref, turned(qkv_ref[1], "hlhl"))
    keep(g_ref, turned(grad_ref[...], "hhll"))
    keep(v_ref, turned(qkv_ref[2], "hlhl"))
    bias = wide(bias_ref[...])
    dqkv_ref[1] = jnp.zeros((PATCH, WIDTH), F32)
    dqkv_ref[2] = jnp.zeros((PATCH, WIDTH), F32)

    def one(head, carry):
        mask = head_mask(head)
        rows = pl.ds(pl.multiple_of(head * HEAD, HEAD), HEAD)
        scores = mm(of_head(k_ref, head), of_head(q_ref, head), NT) + bias
        probs = jnp.exp2(scores - lse_ref[pl.ds(head, 1), :])
        ph, plo = split(probs)
        grad_probs = mm(of_head(v_ref, head), of_head(g_ref, head), NT)
        gh, gl = split(jnp.where(mask, grad_ref[...], 0.0))
        both = mm(ph, jnp.concatenate([gh, gl], axis=1))
        dqkv_ref[2] += both[:, :WIDTH] + both[:, WIDTH:] + mm(plo, gh)
        inner = jnp.sum(gt_ref[rows, :] * att_ref[rows, :], axis=0, keepdims=True)
        grad_scores = probs * (grad_probs - inner)
        sh, sl = split(grad_scores)
        qh, ql = split(jnp.where(mask, qkv_ref[0] * SCALE, 0.0))
        both = mm(sh, jnp.concatenate([qh, ql], axis=1))
        dqkv_ref[1] += both[:, :WIDTH] + both[:, WIDTH:] + mm(sl, qh)
        kh, kl = split(kt_ref[rows, :] * SCALE)
        both = mm(jnp.concatenate([kh, kl], axis=0), sh)
        dqt_ref[rows, :] = both[:HEAD] + both[HEAD:] + mm(kh, sl)
        return carry

    lax.fori_loop(0, HERE, one, 0, unroll=True)
    dqkv_ref[0] = jnp.transpose(dqt_ref[...])


def weights_kernel(
    core_ref, head_ref, x_ref, dqkv_ref, att_ref, before_ref, cot_ref, cot1_ref, cot2_ref, cot3_ref, after_ref, keep_ref, send_ref
):
    del after_ref
    second = core_ref[0] == 1

    def put(block, grads):
        top, bottom = grads[:SIDE], grads[SIDE:]
        keep_ref[block] = jnp.where(second, bottom, top)
        send_ref[block] = jnp.where(second, top, bottom)

    x = split(jnp.concatenate([x_ref[part] for part in range(D // WIDTH)], axis=1))
    for t in range(3):
        grads = jnp.transpose(mm3(split(jnp.transpose(dqkv_ref[t])), x))
        for part in range(D // WIDTH):
            put(t * (D // WIDTH) + part, grads[part * WIDTH : (part + 1) * WIDTH])
    cots = [cot_ref, cot1_ref, cot2_ref, cot3_ref]
    cots = [jnp.concatenate([before_ref[s], ref[:HALF]], axis=0) for s, ref in enumerate(cots)]
    grads = mm3(split(att_ref[...]), split(jnp.concatenate(cots, axis=1)))
    for s in range(D // WIDTH):
        part = along(head_ref[0] + (D // WIDTH - s))[0]
        put(3 * (D // WIDTH) + part, grads[:, s * WIDTH : (s + 1) * WIDTH])


def rows_kernel(dqkv_ref, win_ref, dx_ref, done_ref):
    done_ref[...] = jnp.zeros_like(done_ref)
    grads = split(jnp.concatenate([dqkv_ref[t] for t in range(3)], axis=1))
    for part in range(D // WIDTH):
        rows = slice(part * WIDTH, (part + 1) * WIDTH)
        win = jnp.concatenate([win_ref[t, rows] for t in range(3)], axis=1)
        dx_ref[part] = mm3(grads, split(win), NT)


def call(kernel, outs, *args, scratch=(), sems=(), scalars=0, held=0, sent=0, room=8, flops=10**9):
    size = sum(math.prod(a.shape) * 4 for a in (*args, *outs))
    vmem = pl.BlockSpec(memory_space=pltpu.VMEM)
    hbm = pl.BlockSpec(memory_space=pltpu.HBM)
    return pl.pallas_call(
        kernel,
        out_shape=tuple(jax.ShapeDtypeStruct(o, F32) for o in [x.shape for x in outs]),
        in_specs=[pl.BlockSpec(memory_space=pltpu.SMEM)] * scalars
        + [hbm] * held
        + [vmem] * (len(args) - scalars - held),
        out_specs=tuple([hbm] * sent + [vmem] * (len(outs) - sent)),
        scratch_shapes=[pltpu.VMEM(x, F32) if isinstance(x, tuple) else x for x in scratch]
        + [pltpu.SemaphoreType.DMA(n) for n in sems],
        compiler_params=pltpu.CompilerParams(vmem_limit_bytes=room * 2**20),
        cost_estimate=pl.CostEstimate(flops=flops, bytes_accessed=size, transcendentals=0),
    )(*args)


def of(*shape):
    return jax.ShapeDtypeStruct(shape, F32)


def swap(x, axis):
    return lax.all_to_all(x, axis, split_axis=0, concat_axis=0, tiled=True)


def shards(features, input_proj, output_proj, destination, real_points, cotangent):
    peers = lax.axis_size(CURVE)
    each = PATCH // peers
    up = [(i, (i + 1) % peers) for i in range(peers)]
    down = [(j, i) for i, j in up]
    heads = lax.axis_size("head")
    head = lax.axis_index("head").astype(jnp.int32).reshape(1)
    core = lax.axis_index("core").astype(jnp.int32).reshape(1)

    def ahead(x, step):
        return lax.ppermute(x, "head", [(i, (i + step) % heads) for i in range(heads)])

    def exchange(message):
        rows = message.shape[0]
        return swap(message.reshape(rows, 1, WIDTH), CURVE).reshape(rows, WIDTH)

    message, index = call(
        functools.partial(sort_kernel, each), [of(PATCH + peers, WIDTH), of(1, PATCH)],
        destination.reshape(1, PATCH), features,
    )
    arrived = exchange(message)
    cots = [cotangent] + [ahead(cotangent, s) for s in (1, 2, 3)]
    win = jnp.transpose(input_proj, (1, 0, 2))
    valid = jnp.concatenate([lax.ppermute(real_points[HALF:], CURVE, up), real_points[:HALF]], axis=0)
    valid = valid.reshape(1, PATCH)
    low, high, position, bias = call(
        functools.partial(place_kernel, each),
        [of(HALF, WIDTH), of(HALF, WIDTH), of(1, PATCH), of(PATCH, WIDTH)], *cots[1:], arrived, valid, held=3,
    )
    before = lax.ppermute(jnp.stack([c[HALF:] for c in cots]), CURVE, up)
    x = jnp.concatenate([lax.ppermute(high, CURVE, up), low], axis=0)
    x = jnp.broadcast_to(x[None], (D // WIDTH, PATCH, WIDTH))
    x = swap(x.reshape(-1, WIDTH), "head").reshape(D // WIDTH, PATCH, WIDTH)
    qkv, attended, lse = call(
        forward_kernel,
        [of(3, PATCH, WIDTH), of(WIDTH, PATCH), of(HERE, PATCH)],
        x, win, bias, scratch=[(WIDTH, PATCH)] + [(HERE, PATCH, WIDTH)] * 2, room=24,
    )
    (dqkv,) = call(
        backward_kernel, [of(3, PATCH, WIDTH)], head, qkv, attended, lse, before, *cots, output_proj, bias, scalars=1,
        scratch=[(WIDTH, PATCH)] * 3 + [(PATCH, WIDTH)] + [(HERE, PATCH, WIDTH)] * 4, room=24,
    )
    dx, done = call(
        rows_kernel, [of(D // WIDTH, PATCH, WIDTH), of(8, WIDTH)], dqkv, win
    )
    dx = swap(dx.reshape(-1, WIDTH), "head").reshape(D // WIDTH, PATCH, WIDTH)
    dx_early, dx_late = call(add_kernel, [of(HALF, WIDTH)] * 2, dx)
    keep, send = call(
        weights_kernel, [of(BLOCKS, SIDE, WIDTH)] * 2, core, head, x, dqkv, attended, before, *cots, done, scalars=2
    )
    out = call(output_kernel, [of(PATCH, WIDTH)] * heads, head, attended, output_proj, done, scalars=1)
    out = [out[0]] + [ahead(out[s], s) for s in (1, 2, 3)]
    out_early, out_late = call(sum_kernel, [of(HALF, WIDTH)] * 2, *out)
    sums = keep + lax.ppermute(send, "core", [(0, 1), (1, 0)])
    sums, dx_early = lax.optimization_barrier((sums, dx_early))
    sums = swap(sums.reshape(-1, WIDTH), PLANE).reshape(BLOCKS, SIDE, WIDTH)
    (message,) = call(
        functools.partial(pack_kernel, each), [of(peers * (each + ADDED), WIDTH)],
        position, dx_late, lax.ppermute(dx_early, CURVE, down), sums,
    )
    message = exchange(message)
    (sums,) = call(
        functools.partial(unpack_kernel, each), [of(BLOCKS, SIDE, WIDTH)], message,
        sent=1, scratch=[(SIDE, WIDTH)], sems=[(BLOCKS,)],
    )
    sums, out_early = lax.optimization_barrier((sums, out_early))
    sums = swap(sums.reshape(-1, WIDTH), PLANE).reshape(BLOCKS, SIDE, WIDTH)
    branch_out = jnp.concatenate([out_late, lax.ppermute(out_early, CURVE, down)], axis=0)
    sums, message, branch_out = lax.optimization_barrier((sums, message, branch_out))
    (grad_features,) = call(functools.partial(unsort_kernel, each), [of(PATCH, WIDTH)], index, message)
    grad_inproj, grad_outproj = call(
        finish_kernel, [of(3, D, WIDTH), of(WIDTH, D)],
        core, sums, lax.ppermute(sums, "core", [(0, 1), (1, 0)]), scalars=1,
        scratch=[(D // WIDTH, WIDTH, WIDTH)],
    )
    return (branch_out, grad_features, jnp.transpose(grad_inproj, (1, 0, 2)), grad_outproj)


def solution(mesh):
    curve, head = mesh.devices.shape
    sizes = (curve // 32, 4, 4, 2)
    fine = jax.sharding.Mesh(mesh.devices.reshape(*sizes, head), CURVE + ("head",))
    return jax.shard_map(
        shards,
        mesh=fine,
        in_specs=(
            P(CURVE, "head"),
            P(None, None, "head"),
            P("head", None),
            P(CURVE),
            P(CURVE),
            P(CURVE, "head"),
        ),
        out_specs=(P(CURVE, "head"), P(CURVE, "head"), P(None, None, "head"), P("head", None)),
        check_vma=False,
    )
```

```python
import functools
import math

import jax
import jax.numpy as jnp
from jax import lax
from jax.experimental import pallas as pl
from jax.experimental.pallas import tpu as pltpu
from jax.sharding import PartitionSpec as P

D = 512
HEADS = 16
PATCH = 512
HALF = PATCH // 2
HEAD = D // HEADS
WIDTH = 128
HERE = WIDTH // HEAD
CURVE = ("far", "near", "x", "core")
PLANE = ("near", "x")
BLOCKS = 16
SIDE = WIDTH // 2
ADDED = 2
BF = jnp.bfloat16
F32 = jnp.float32
SCALE = 1.0 / math.sqrt(HEAD)
LOG2E = math.log2(math.e)

NN = (((1,), (0,)), ((), ()))
NT = (((1,), (1,)), ((), ()))


def mm(a, b, dims=NN):
    return lax.dot_general(a, b, dims, preferred_element_type=F32)


def split(x):
    high = x.astype(BF)
    return high, (x - high.astype(F32)).astype(BF)


def split3(x):
    high, rest = x.astype(BF), None
    rest = x - high.astype(F32)
    mid = rest.astype(BF)
    return high, mid, (rest - mid.astype(F32)).astype(BF)


def mm3(a, b, dims=NN):
    (ah, al), (bh, bl) = a, b
    (left,), (right,) = dims[0]
    return mm(jnp.concatenate([ah, al, ah], axis=left), jnp.concatenate([bh, bh, bl], axis=right), dims)


def select_rows(pick, x):
    high, mid, low = split3(x)
    return mm(pick, high) + (mm(pick, mid) + mm(pick, low))


def column(row):
    return jnp.transpose(jnp.broadcast_to(row, (WIDTH, row.shape[1])))


def wide(col, width=PATCH):
    return jnp.concatenate([col] * (width // WIDTH), axis=1)


def iota(dim, shape=(PATCH, PATCH)):
    return lax.broadcasted_iota(jnp.int32, shape, dim).astype(F32)


def one_hot(condition):
    return jnp.where(condition, 1.0, 0.0).astype(BF)


def every(ref, first, step):
    return ref[pl.ds(first, ref.shape[0] // step, stride=step), :]


def index_kernel(each, dest_ref, index_ref, lists_ref):
    peers = PATCH // each
    dest = dest_ref[...]
    block = dest // PATCH
    local = (dest - block * PATCH).astype(F32)
    block = block.astype(F32)
    same = (wide(column(block)) == block) & (iota(0) < iota(1))
    rank = jnp.sum(jnp.where(same, 1.0, 0.0), axis=0, keepdims=True)
    index_ref[...] = rank * peers + block
    high, low = split(jnp.where(iota(1, (PATCH, WIDTH)) == column(rank), column(local), 0.0))
    mine = one_hot(iota(0, (peers, PATCH)) == block)
    lists_ref[...] = mm(mine, high) + mm(mine, low)


def sort_kernel(each, index_ref, lists_ref, feat_ref, message_ref):
    peers = PATCH // each
    rows = select_rows(one_hot(iota(0) == index_ref[...]), feat_ref[...])
    for turn in range(each):
        message_ref[pl.ds(turn, peers, stride=each + 1), :] = rows[turn * peers : (turn + 1) * peers]
    message_ref[pl.ds(each, peers, stride=each + 1), :] = lists_ref[...]


def place_kernel(each, after1_ref, after2_ref, after3_ref, message_ref, low_ref, high_ref, position_ref):
    del after1_ref, after2_ref, after3_ref
    turned = jnp.transpose(every(message_ref, each, each + 1))
    position = jnp.concatenate([turned[turn : turn + 1] for turn in range(each)], axis=1)
    position_ref[...] = position
    arrived = jnp.concatenate([every(message_ref, turn, each + 1) for turn in range(each)], axis=0)
    placed = select_rows(one_hot(iota(0) == position), arrived)
    low_ref[...] = placed[:HALF]
    high_ref[...] = placed[HALF:]


def add_kernel(parts_ref, early_ref, late_ref):
    total = parts_ref[0] + parts_ref[1] + (parts_ref[2] + parts_ref[3])
    early_ref[...] = total[:HALF]
    late_ref[...] = total[HALF:]


def pack_kernel(each, position_ref, low_ref, high_ref, sums_ref, message_ref):
    peers = PATCH // each
    size = each + ADDED
    grads = jnp.concatenate([low_ref[...], high_ref[...]], axis=0)
    rows = select_rows(one_hot(wide(column(position_ref[...])) == iota(1)), grads)
    for turn in range(each):
        message_ref[pl.ds(turn, peers, stride=size), :] = rows[turn * peers : (turn + 1) * peers]
    sums = sums_ref[0]
    for part in range(1, sums_ref.shape[0]):
        sums += sums_ref[part]
    near = SIDE // ADDED
    for turn in range(ADDED):
        for core in range(2):
            first = turn * near + core * BLOCKS
            rows = jnp.concatenate([sums[first : first + BLOCKS]] * (peers // near), axis=0)
            message_ref[pl.ds(core * size + each + turn, peers // 2, stride=2 * size), :] = rows


def unpack_kernel(each, message_ref, out_hbm, sums_ref, sems):
    near = SIDE // ADDED
    for turn in range(ADDED):
        rows = every(message_ref, each + turn, each + ADDED)
        total = rows[:near]
        for far in range(1, rows.shape[0] // near):
            total += rows[far * near : (far + 1) * near]
        sums_ref[turn * near : (turn + 1) * near] = total
    copies = [pltpu.make_async_copy(sums_ref, out_hbm.at[i], sems.at[i]) for i in range(BLOCKS)]
    for copy in copies:
        copy.start()
    for copy in copies:
        copy.wait()


def unsort_kernel(each, index_ref, message_ref, out_ref):
    returned = jnp.concatenate([every(message_ref, turn, each + ADDED) for turn in range(each)], axis=0)
    out_ref[...] = select_rows(one_hot(wide(column(index_ref[...])) == iota(1)), returned)


def finish_kernel(core_ref, mine_ref, other_ref, din_ref, dout_ref):
    core = core_ref[0]
    near = SIDE // ADDED
    for own, ref in ((core, mine_ref), (1 - core, other_ref)):
        for block in range(BLOCKS):
            t, part = divmod(block, D // WIDTH)
            for side in range(2):
                for turn in range(ADDED):
                    got = ref[:, turn * near + 2 * block + side, :]
                    first = pl.multiple_of(side * SIDE + turn * near + own * BLOCKS, BLOCKS)
                    if t < 3:
                        din_ref[t, pl.ds(part * WIDTH + first, BLOCKS), :] = got
                    else:
                        dout_ref[pl.ds(first, BLOCKS), part * WIDTH : (part + 1) * WIDTH] = got


def head_mask(head):
    lanes = lax.broadcasted_iota(jnp.int32, (PATCH, WIDTH), 1)
    return (lanes // HEAD) == head


def turned(x, order):
    high, low = split(x)
    parts = {"h": high.astype(F32), "l": low.astype(F32)}
    return [parts[o] if not i else pltpu.roll(parts[o], i * HEAD, 1) for i, o in enumerate(order)]


def of_head(refs, head):
    lanes = lax.broadcasted_iota(jnp.int32, (PATCH, WIDTH), 1)
    turn = (lanes // HEAD - head) & (HERE - 1)
    x = refs[0]
    for i in range(1, HERE):
        x = jnp.where(turn == i, refs[i], x)
    return x.astype(BF)


def keep(ref, parts):
    for i, part in enumerate(parts):
        ref[i] = part


def forward_kernel(x_ref, win_ref, valid_ref, qkv_ref, att_ref, lse_ref, vt_ref, q_ref, k_ref):
    x = jnp.concatenate([x_ref[part] for part in range(D // WIDTH)], axis=1)
    win = jnp.concatenate([win_ref[t] for t in range(3)], axis=1)
    qkv = mm3(split(x), split(win))
    for t in range(3):
        qkv_ref[t] = qkv[:, t * WIDTH : (t + 1) * WIDTH]
    vt_ref[...] = jnp.transpose(qkv_ref[2])
    keep(q_ref, turned(qkv_ref[0] * (SCALE * LOG2E), "hhll"))
    keep(k_ref, turned(qkv_ref[1], "hlhl"))
    bias = wide(column(jnp.where(valid_ref[...] > 0, 0.0, -jnp.inf)))

    def one(head, carry):
        scores = mm(of_head(k_ref, head), of_head(q_ref, head), NT) + bias
        top = jnp.max(scores, axis=0, keepdims=True)
        weights = jnp.exp2(scores - top)
        total = jnp.sum(weights, axis=0, keepdims=True)
        rows = pl.ds(pl.multiple_of(head * HEAD, HEAD), HEAD)
        vh, vl = split(vt_ref[rows, :])
        wh, wl = split(weights)
        both = mm(jnp.concatenate([vh, vl], axis=0), wh)
        attended = both[:HEAD] + both[HEAD:] + mm(vh, wl)
        att_ref[rows, :] = attended / total
        lse_ref[pl.ds(head, 1), :] = top + jnp.log2(total)
        return carry

    lax.fori_loop(0, HERE, one, 0, unroll=True)


def cot_kernel(head_ref, cot_ref, cot1_ref, cot2_ref, cot3_ref, wout_ref, early_ref, late_ref, send_ref):
    cots = [ref[...] for ref in (cot_ref, cot1_ref, cot2_ref, cot3_ref)]
    wout = [wout_ref[:, along(head_ref[0] + (D // WIDTH - s))[1]] for s in range(D // WIDTH)]
    grads = mm3(split(jnp.concatenate(cots, axis=1)), split(jnp.concatenate(wout, axis=1)), NT)
    early_ref[...] = grads[:HALF]
    late_ref[...] = grads[HALF:]
    for s, cot in enumerate(cots):
        send_ref[s] = cot[HALF:]


def along(step):
    part = lax.rem(step, D // WIDTH)
    return part, pl.ds(pl.multiple_of(part * WIDTH, WIDTH), WIDTH)


def output_kernel(head_ref, att_ref, wout_ref, after_ref, *out_refs):
    del after_ref
    attended = split(jnp.transpose(att_ref[...]))
    for step, out_ref in enumerate(out_refs):
        out_ref[...] = mm3(attended, split(wout_ref[:, along(head_ref[0] + step)[1]]))


def sum_kernel(first_ref, second_ref, third_ref, fourth_ref, early_ref, late_ref):
    total = first_ref[...] + second_ref[...] + (third_ref[...] + fourth_ref[...])
    early_ref[...] = total[:HALF]
    late_ref[...] = total[HALF:]


def backward_kernel(
    qkv_ref, att_ref, lse_ref, before_ref, early_ref, valid_ref,
    dqkv_ref, kt_ref, gt_ref, dqt_ref, grad_ref, q_ref, k_ref, v_ref, g_ref,
):
    grad_ref[:HALF] = before_ref[...]
    grad_ref[HALF:] = early_ref[...]
    kt_ref[...] = jnp.transpose(qkv_ref[1])
    gt_ref[...] = jnp.transpose(grad_ref[...])
    keep(q_ref, turned(qkv_ref[0] * (SCALE * LOG2E), "hhll"))
    keep(k_ref, turned(qkv_ref[1], "hlhl"))
    keep(g_ref, turned(grad_ref[...], "hhll"))
    keep(v_ref, turned(qkv_ref[2], "hlhl"))
    bias = wide(column(jnp.where(valid_ref[...] > 0, 0.0, -jnp.inf)))
    dqkv_ref[1] = jnp.zeros((PATCH, WIDTH), F32)
    dqkv_ref[2] = jnp.zeros((PATCH, WIDTH), F32)

    def one(head, carry):
        mask = head_mask(head)
        rows = pl.ds(pl.multiple_of(head * HEAD, HEAD), HEAD)
        scores = mm(of_head(k_ref, head), of_head(q_ref, head), NT) + bias
        probs = jnp.exp2(scores - lse_ref[pl.ds(head, 1), :])
        ph, plo = split(probs)
        grad_probs = mm(of_head(v_ref, head), of_head(g_ref, head), NT)
        gh, gl = split(jnp.where(mask, grad_ref[...], 0.0))
        both = mm(ph, jnp.concatenate([gh, gl], axis=1))
        dqkv_ref[2] += both[:, :WIDTH] + both[:, WIDTH:] + mm(plo, gh)
        inner = jnp.sum(gt_ref[rows, :] * att_ref[rows, :], axis=0, keepdims=True)
        grad_scores = probs * (grad_probs - inner)
        sh, sl = split(grad_scores)
        qh, ql = split(jnp.where(mask, qkv_ref[0] * SCALE, 0.0))
        both = mm(sh, jnp.concatenate([qh, ql], axis=1))
        dqkv_ref[1] += both[:, :WIDTH] + both[:, WIDTH:] + mm(sl, qh)
        kh, kl = split(kt_ref[rows, :] * SCALE)
        both = mm(jnp.concatenate([kh, kl], axis=0), sh)
        dqt_ref[rows, :] = both[:HEAD] + both[HEAD:] + mm(kh, sl)
        return carry

    lax.fori_loop(0, HERE, one, 0, unroll=True)
    dqkv_ref[0] = jnp.transpose(dqt_ref[...])


def weights_kernel(
    core_ref, head_ref, x_ref, dqkv_ref, att_ref, before_ref, cot_ref, cot1_ref, cot2_ref, cot3_ref, after_ref, keep_ref, send_ref
):
    del after_ref
    second = core_ref[0] == 1

    def put(block, grads):
        top, bottom = grads[:SIDE], grads[SIDE:]
        keep_ref[block] = jnp.where(second, bottom, top)
        send_ref[block] = jnp.where(second, top, bottom)

    x = split(jnp.concatenate([x_ref[part] for part in range(D // WIDTH)], axis=1))
    for t in range(3):
        grads = jnp.transpose(mm3(split(jnp.transpose(dqkv_ref[t])), x))
        for part in range(D // WIDTH):
            put(t * (D // WIDTH) + part, grads[part * WIDTH : (part + 1) * WIDTH])
    cots = [cot_ref, cot1_ref, cot2_ref, cot3_ref]
    cots = [jnp.concatenate([before_ref[s], ref[:HALF]], axis=0) for s, ref in enumerate(cots)]
    grads = mm3(split(att_ref[...]), split(jnp.concatenate(cots, axis=1)))
    for s in range(D // WIDTH):
        part = along(head_ref[0] + (D // WIDTH - s))[0]
        put(3 * (D // WIDTH) + part, grads[:, s * WIDTH : (s + 1) * WIDTH])


def rows_kernel(dqkv_ref, win_ref, dx_ref, done_ref):
    done_ref[...] = jnp.zeros_like(done_ref)
    grads = split(jnp.concatenate([dqkv_ref[t] for t in range(3)], axis=1))
    for part in range(D // WIDTH):
        rows = slice(part * WIDTH, (part + 1) * WIDTH)
        win = jnp.concatenate([win_ref[t, rows] for t in range(3)], axis=1)
        dx_ref[part] = mm3(grads, split(win), NT)


def call(kernel, outs, *args, scratch=(), sems=(), scalars=0, held=0, sent=0, room=8, flops=10**9):
    size = sum(math.prod(a.shape) * 4 for a in (*args, *outs))
    vmem = pl.BlockSpec(memory_space=pltpu.VMEM)
    hbm = pl.BlockSpec(memory_space=pltpu.HBM)
    return pl.pallas_call(
        kernel,
        out_shape=tuple(jax.ShapeDtypeStruct(o, F32) for o in [x.shape for x in outs]),
        in_specs=[pl.BlockSpec(memory_space=pltpu.SMEM)] * scalars
        + [hbm] * held
        + [vmem] * (len(args) - scalars - held),
        out_specs=tuple([hbm] * sent + [vmem] * (len(outs) - sent)),
        scratch_shapes=[pltpu.VMEM(x, F32) if isinstance(x, tuple) else x for x in scratch]
        + [pltpu.SemaphoreType.DMA(n) for n in sems],
        compiler_params=pltpu.CompilerParams(vmem_limit_bytes=room * 2**20),
        cost_estimate=pl.CostEstimate(flops=flops, bytes_accessed=size, transcendentals=0),
    )(*args)


def of(*shape):
    return jax.ShapeDtypeStruct(shape, F32)


def swap(x, axis):
    return lax.all_to_all(x, axis, split_axis=0, concat_axis=0, tiled=True)


def shards(features, input_proj, output_proj, destination, real_points, cotangent):
    peers = lax.axis_size(CURVE)
    each = PATCH // peers
    up = [(i, (i + 1) % peers) for i in range(peers)]
    down = [(j, i) for i, j in up]
    heads = lax.axis_size("head")
    head = lax.axis_index("head").astype(jnp.int32).reshape(1)
    core = lax.axis_index("core").astype(jnp.int32).reshape(1)

    def ahead(x, step):
        return lax.ppermute(x, "head", [(i, (i + step) % heads) for i in range(heads)])

    def exchange(message):
        rows = message.shape[0]
        return swap(message.reshape(rows, 1, WIDTH), CURVE).reshape(rows, WIDTH)

    index, lists = call(
        functools.partial(index_kernel, each), [of(1, PATCH), of(peers, WIDTH)], destination.reshape(1, PATCH)
    )
    (message,) = call(functools.partial(sort_kernel, each), [of(PATCH + peers, WIDTH)], index, lists, features)
    arrived = exchange(message)
    cots = [cotangent] + [ahead(cotangent, s) for s in (1, 2, 3)]
    win = jnp.transpose(input_proj, (1, 0, 2))
    valid = jnp.concatenate([lax.ppermute(real_points[HALF:], CURVE, up), real_points[:HALF]], axis=0)
    valid = valid.reshape(1, PATCH)
    low, high, position = call(
        functools.partial(place_kernel, each),
        [of(HALF, WIDTH), of(HALF, WIDTH), of(1, PATCH)], *cots[1:], arrived, held=3,
    )
    grad_early, grad_late, cot_late = call(
        cot_kernel, [of(HALF, WIDTH), of(HALF, WIDTH), of(heads, HALF, WIDTH)], head, *cots, output_proj, scalars=1,
    )
    grad_before = lax.ppermute(grad_late, CURVE, up)
    before = lax.ppermute(cot_late, CURVE, up)
    x = jnp.concatenate([lax.ppermute(high, CURVE, up), low], axis=0)
    x = jnp.broadcast_to(x[None], (D // WIDTH, PATCH, WIDTH))
    x = swap(x.reshape(-1, WIDTH), "head").reshape(D // WIDTH, PATCH, WIDTH)
    qkv, attended, lse = call(
        forward_kernel,
        [of(3, PATCH, WIDTH), of(WIDTH, PATCH), of(HERE, PATCH)],
        x, win, valid, scratch=[(WIDTH, PATCH)] + [(HERE, PATCH, WIDTH)] * 2, room=24,
    )
    (dqkv,) = call(
        backward_kernel, [of(3, PATCH, WIDTH)], qkv, attended, lse, grad_before, grad_early, valid,
        scratch=[(WIDTH, PATCH)] * 3 + [(PATCH, WIDTH)] + [(HERE, PATCH, WIDTH)] * 4, room=24,
    )
    dx, done = call(
        rows_kernel, [of(D // WIDTH, PATCH, WIDTH), of(8, WIDTH)], dqkv, win
    )
    dx = swap(dx.reshape(-1, WIDTH), "head").reshape(D // WIDTH, PATCH, WIDTH)
    dx_early, dx_late = call(add_kernel, [of(HALF, WIDTH)] * 2, dx)
    keep, send = call(
        weights_kernel, [of(BLOCKS, SIDE, WIDTH)] * 2, core, head, x, dqkv, attended, before, *cots, done, scalars=2
    )
    out = call(output_kernel, [of(PATCH, WIDTH)] * heads, head, attended, output_proj, done, scalars=1)
    out = [out[0]] + [ahead(out[s], s) for s in (1, 2, 3)]
    out_early, out_late = call(sum_kernel, [of(HALF, WIDTH)] * 2, *out)
    sums = keep + lax.ppermute(send, "core", [(0, 1), (1, 0)])
    sums, dx_early = lax.optimization_barrier((sums, dx_early))
    sums = swap(sums.reshape(-1, WIDTH), PLANE).reshape(BLOCKS, SIDE, WIDTH)
    (message,) = call(
        functools.partial(pack_kernel, each), [of(peers * (each + ADDED), WIDTH)],
        position, dx_late, lax.ppermute(dx_early, CURVE, down), sums,
    )
    message = exchange(message)
    (sums,) = call(
        functools.partial(unpack_kernel, each), [of(BLOCKS, SIDE, WIDTH)], message,
        sent=1, scratch=[(SIDE, WIDTH)], sems=[(BLOCKS,)],
    )
    sums, out_early = lax.optimization_barrier((sums, out_early))
    sums = swap(sums.reshape(-1, WIDTH), PLANE).reshape(BLOCKS, SIDE, WIDTH)
    branch_out = jnp.concatenate([out_late, lax.ppermute(out_early, CURVE, down)], axis=0)
    sums, message, branch_out = lax.optimization_barrier((sums, message, branch_out))
    (grad_features,) = call(functools.partial(unsort_kernel, each), [of(PATCH, WIDTH)], index, message)
    grad_inproj, grad_outproj = call(
        finish_kernel, [of(3, D, WIDTH), of(WIDTH, D)],
        core, sums, lax.ppermute(sums, "core", [(0, 1), (1, 0)]), scalars=1,
    )
    return (branch_out, grad_features, jnp.transpose(grad_inproj, (1, 0, 2)), grad_outproj)


def solution(mesh):
    curve, head = mesh.devices.shape
    sizes = (curve // 32, 4, 4, 2)
    fine = jax.sharding.Mesh(mesh.devices.reshape(*sizes, head), CURVE + ("head",))
    return jax.shard_map(
        shards,
        mesh=fine,
        in_specs=(
            P(CURVE, "head"),
            P(None, None, "head"),
            P("head", None),
            P(CURVE),
            P(CURVE),
            P(CURVE, "head"),
        ),
        out_specs=(P(CURVE, "head"), P(CURVE, "head"), P(None, None, "head"), P("head", None)),
        check_vma=False,
    )
```

```python
import functools
import math

import jax
import jax.numpy as jnp
from jax import lax
from jax.experimental import pallas as pl
from jax.experimental.pallas import tpu as pltpu
from jax.sharding import PartitionSpec as P

D = 512
HEADS = 16
PATCH = 512
HALF = PATCH // 2
HEAD = D // HEADS
WIDTH = 128
HERE = WIDTH // HEAD
CURVE = ("far", "near", "x", "core")
PLANE = ("near", "x")
BLOCKS = 16
SIDE = WIDTH // 2
ADDED = 2
BF = jnp.bfloat16
F32 = jnp.float32
SCALE = 1.0 / math.sqrt(HEAD)
LOG2E = math.log2(math.e)

NN = (((1,), (0,)), ((), ()))
NT = (((1,), (1,)), ((), ()))


def mm(a, b, dims=NN):
    return lax.dot_general(a, b, dims, preferred_element_type=F32)


def split(x):
    high = x.astype(BF)
    return high, (x - high.astype(F32)).astype(BF)


def split3(x):
    high, rest = x.astype(BF), None
    rest = x - high.astype(F32)
    mid = rest.astype(BF)
    return high, mid, (rest - mid.astype(F32)).astype(BF)


def mm3(a, b, dims=NN):
    (ah, al), (bh, bl) = a, b
    (left,), (right,) = dims[0]
    return mm(jnp.concatenate([ah, al, ah], axis=left), jnp.concatenate([bh, bh, bl], axis=right), dims)


def select_rows(pick, x):
    high, mid, low = split3(x)
    return mm(pick, high) + (mm(pick, mid) + mm(pick, low))


def column(row):
    return jnp.transpose(jnp.broadcast_to(row, (WIDTH, row.shape[1])))


def wide(col, width=PATCH):
    return jnp.concatenate([col] * (width // WIDTH), axis=1)


def iota(dim, shape=(PATCH, PATCH)):
    return lax.broadcasted_iota(jnp.int32, shape, dim).astype(F32)


def one_hot(condition):
    return jnp.where(condition, 1.0, 0.0).astype(BF)


def every(ref, first, step):
    return ref[pl.ds(first, ref.shape[0] // step, stride=step), :]


def index_kernel(each, dest_ref, index_ref, lists_ref):
    peers = PATCH // each
    dest = dest_ref[...]
    block = dest // PATCH
    local = (dest - block * PATCH).astype(F32)
    block = block.astype(F32)
    same = (wide(column(block)) == block) & (iota(0) < iota(1))
    rank = jnp.sum(jnp.where(same, 1.0, 0.0), axis=0, keepdims=True)
    index_ref[...] = rank * peers + block
    high, low = split(jnp.where(iota(1, (PATCH, WIDTH)) == column(rank), column(local), 0.0))
    mine = one_hot(iota(0, (peers, PATCH)) == block)
    lists_ref[...] = mm(mine, high) + mm(mine, low)


def sort_kernel(each, index_ref, lists_ref, feat_ref, message_ref):
    peers = PATCH // each
    rows = select_rows(one_hot(iota(0) == index_ref[...]), feat_ref[...])
    for turn in range(each):
        message_ref[pl.ds(turn, peers, stride=each + 1), :] = rows[turn * peers : (turn + 1) * peers]
    message_ref[pl.ds(each, peers, stride=each + 1), :] = lists_ref[...]


def place_kernel(each, after1_ref, after2_ref, after3_ref, message_ref, low_ref, high_ref, position_ref):
    del after1_ref, after2_ref, after3_ref
    turned = jnp.transpose(every(message_ref, each, each + 1))
    position = jnp.concatenate([turned[turn : turn + 1] for turn in range(each)], axis=1)
    position_ref[...] = position
    arrived = jnp.concatenate([every(message_ref, turn, each + 1) for turn in range(each)], axis=0)
    placed = select_rows(one_hot(iota(0) == position), arrived)
    low_ref[...] = placed[:HALF]
    high_ref[...] = placed[HALF:]


def add_kernel(parts_ref, early_ref, late_ref):
    total = parts_ref[0] + parts_ref[1] + (parts_ref[2] + parts_ref[3])
    early_ref[...] = total[:HALF]
    late_ref[...] = total[HALF:]


def pack_kernel(each, position_ref, low_ref, high_ref, sums_ref, message_ref):
    peers = PATCH // each
    size = each + ADDED
    grads = jnp.concatenate([low_ref[...], high_ref[...]], axis=0)
    rows = select_rows(one_hot(wide(column(position_ref[...])) == iota(1)), grads)
    for turn in range(each):
        message_ref[pl.ds(turn, peers, stride=size), :] = rows[turn * peers : (turn + 1) * peers]
    sums = sums_ref[0]
    for part in range(1, sums_ref.shape[0]):
        sums += sums_ref[part]
    near = SIDE // ADDED
    for turn in range(ADDED):
        for core in range(2):
            first = turn * near + core * BLOCKS
            rows = jnp.concatenate([sums[first : first + BLOCKS]] * (peers // near), axis=0)
            message_ref[pl.ds(core * size + each + turn, peers // 2, stride=2 * size), :] = rows


def unpack_kernel(each, message_ref, out_hbm, sums_ref, sems):
    near = SIDE // ADDED
    for turn in range(ADDED):
        rows = every(message_ref, each + turn, each + ADDED)
        total = rows[:near]
        for far in range(1, rows.shape[0] // near):
            total += rows[far * near : (far + 1) * near]
        sums_ref[turn * near : (turn + 1) * near] = total
    copies = [pltpu.make_async_copy(sums_ref, out_hbm.at[i], sems.at[i]) for i in range(BLOCKS)]
    for copy in copies:
        copy.start()
    for copy in copies:
        copy.wait()


def unsort_kernel(each, index_ref, message_ref, out_ref):
    returned = jnp.concatenate([every(message_ref, turn, each + ADDED) for turn in range(each)], axis=0)
    out_ref[...] = select_rows(one_hot(wide(column(index_ref[...])) == iota(1)), returned)


def finish_kernel(core_ref, mine_ref, other_ref, din_ref, dout_ref):
    core = core_ref[0]
    near = SIDE // ADDED
    for own, ref in ((core, mine_ref), (1 - core, other_ref)):
        for block in range(BLOCKS):
            t, part = divmod(block, D // WIDTH)
            for side in range(2):
                for turn in range(ADDED):
                    got = ref[:, turn * near + 2 * block + side, :]
                    first = pl.multiple_of(side * SIDE + turn * near + own * BLOCKS, BLOCKS)
                    if t < 3:
                        din_ref[t, pl.ds(part * WIDTH + first, BLOCKS), :] = got
                    else:
                        dout_ref[pl.ds(first, BLOCKS), part * WIDTH : (part + 1) * WIDTH] = got


def head_mask(head):
    lanes = lax.broadcasted_iota(jnp.int32, (PATCH, WIDTH), 1)
    return (lanes // HEAD) == head


def turned(x, order):
    high, low = split(x)
    parts = {"h": high.astype(F32), "l": low.astype(F32)}
    return [parts[o] if not i else pltpu.roll(parts[o], i * HEAD, 1) for i, o in enumerate(order)]


def of_head(refs, head):
    lanes = lax.broadcasted_iota(jnp.int32, (PATCH, WIDTH), 1)
    turn = (lanes // HEAD - head) & (HERE - 1)
    x = refs[0]
    for i in range(1, HERE):
        x = jnp.where(turn == i, refs[i], x)
    return x.astype(BF)


def keep(ref, parts):
    for i, part in enumerate(parts):
        ref[i] = part


def forward_kernel(x_ref, win_ref, valid_ref, qkv_ref, att_ref, lse_ref, vt_ref, q_ref, k_ref):
    x = jnp.concatenate([x_ref[part] for part in range(D // WIDTH)], axis=1)
    win = jnp.concatenate([win_ref[t] for t in range(3)], axis=1)
    qkv = mm3(split(x), split(win))
    for t in range(3):
        qkv_ref[t] = qkv[:, t * WIDTH : (t + 1) * WIDTH]
    vt_ref[...] = jnp.transpose(qkv_ref[2])
    keep(q_ref, turned(qkv_ref[0] * (SCALE * LOG2E), "hhll"))
    keep(k_ref, turned(qkv_ref[1], "hlhl"))
    bias = wide(column(jnp.where(valid_ref[...] > 0, 0.0, -jnp.inf)))

    def one(head, carry):
        scores = mm(of_head(k_ref, head), of_head(q_ref, head), NT) + bias
        top = jnp.max(scores, axis=0, keepdims=True)
        weights = jnp.exp2(scores - top)
        total = jnp.sum(weights, axis=0, keepdims=True)
        rows = pl.ds(pl.multiple_of(head * HEAD, HEAD), HEAD)
        vh, vl = split(vt_ref[rows, :])
        wh, wl = split(weights)
        both = mm(jnp.concatenate([vh, vl], axis=0), wh)
        attended = both[:HEAD] + both[HEAD:] + mm(vh, wl)
        att_ref[rows, :] = attended / total
        lse_ref[pl.ds(head, 1), :] = top + jnp.log2(total)
        return carry

    lax.fori_loop(0, HERE, one, 0, unroll=True)


def cot_kernel(head_ref, cot_ref, cot1_ref, cot2_ref, cot3_ref, wout_ref, early_ref, late_ref, stay_ref, send_ref):
    cots = [ref[...] for ref in (cot_ref, cot1_ref, cot2_ref, cot3_ref)]
    wout = [wout_ref[:, along(head_ref[0] + (D // WIDTH - s))[1]] for s in range(D // WIDTH)]
    grads = mm3(split(jnp.concatenate(cots, axis=1)), split(jnp.concatenate(wout, axis=1)), NT)
    early_ref[...] = grads[:HALF]
    late_ref[...] = grads[HALF:]
    for s, cot in enumerate(cots):
        stay_ref[s] = cot[:HALF]
        send_ref[s] = cot[HALF:]


def along(step):
    part = lax.rem(step, D // WIDTH)
    return part, pl.ds(pl.multiple_of(part * WIDTH, WIDTH), WIDTH)


def output_kernel(head_ref, att_ref, wout_ref, after_ref, *out_refs):
    del after_ref
    attended = split(jnp.transpose(att_ref[...]))
    for step, out_ref in enumerate(out_refs):
        out_ref[...] = mm3(attended, split(wout_ref[:, along(head_ref[0] + step)[1]]))


def sum_kernel(first_ref, second_ref, third_ref, fourth_ref, early_ref, late_ref):
    total = first_ref[...] + second_ref[...] + (third_ref[...] + fourth_ref[...])
    early_ref[...] = total[:HALF]
    late_ref[...] = total[HALF:]


def backward_kernel(
    qkv_ref, att_ref, lse_ref, before_ref, early_ref, valid_ref,
    dqkv_ref, kt_ref, gt_ref, dqt_ref, grad_ref, q_ref, k_ref, v_ref, g_ref,
):
    grad_ref[:HALF] = before_ref[...]
    grad_ref[HALF:] = early_ref[...]
    kt_ref[...] = jnp.transpose(qkv_ref[1])
    gt_ref[...] = jnp.transpose(grad_ref[...])
    keep(q_ref, turned(qkv_ref[0] * (SCALE * LOG2E), "hhll"))
    keep(k_ref, turned(qkv_ref[1], "hlhl"))
    keep(g_ref, turned(grad_ref[...], "hhll"))
    keep(v_ref, turned(qkv_ref[2], "hlhl"))
    bias = wide(column(jnp.where(valid_ref[...] > 0, 0.0, -jnp.inf)))
    dqkv_ref[1] = jnp.zeros((PATCH, WIDTH), F32)
    dqkv_ref[2] = jnp.zeros((PATCH, WIDTH), F32)

    def one(head, carry):
        mask = head_mask(head)
        rows = pl.ds(pl.multiple_of(head * HEAD, HEAD), HEAD)
        scores = mm(of_head(k_ref, head), of_head(q_ref, head), NT) + bias
        probs = jnp.exp2(scores - lse_ref[pl.ds(head, 1), :])
        ph, plo = split(probs)
        grad_probs = mm(of_head(v_ref, head), of_head(g_ref, head), NT)
        gh, gl = split(jnp.where(mask, grad_ref[...], 0.0))
        both = mm(ph, jnp.concatenate([gh, gl], axis=1))
        dqkv_ref[2] += both[:, :WIDTH] + both[:, WIDTH:] + mm(plo, gh)
        inner = jnp.sum(gt_ref[rows, :] * att_ref[rows, :], axis=0, keepdims=True)
        grad_scores = probs * (grad_probs - inner)
        sh, sl = split(grad_scores)
        qh, ql = split(jnp.where(mask, qkv_ref[0] * SCALE, 0.0))
        both = mm(sh, jnp.concatenate([qh, ql], axis=1))
        dqkv_ref[1] += both[:, :WIDTH] + both[:, WIDTH:] + mm(sl, qh)
        kh, kl = split(kt_ref[rows, :] * SCALE)
        both = mm(jnp.concatenate([kh, kl], axis=0), sh)
        dqt_ref[rows, :] = both[:HEAD] + both[HEAD:] + mm(kh, sl)
        return carry

    lax.fori_loop(0, HERE, one, 0, unroll=True)
    dqkv_ref[0] = jnp.transpose(dqt_ref[...])
    dqkv_ref[3] = jnp.transpose(att_ref[...])


def weights_kernel(core_ref, head_ref, x_ref, dqkv_ref, before_ref, early_ref, after_ref, keep_ref, send_ref):
    del after_ref
    second = core_ref[0] == 1

    def put(block, grads):
        top, bottom = grads[:SIDE], grads[SIDE:]
        keep_ref[block] = jnp.where(second, bottom, top)
        send_ref[block] = jnp.where(second, top, bottom)

    x = split(jnp.concatenate([x_ref[part] for part in range(D // WIDTH)], axis=1))
    for t in range(3):
        grads = jnp.transpose(mm3(split(jnp.transpose(dqkv_ref[t])), x))
        for part in range(D // WIDTH):
            put(t * (D // WIDTH) + part, grads[part * WIDTH : (part + 1) * WIDTH])
    cots = [jnp.concatenate([before_ref[s], early_ref[s]], axis=0) for s in range(D // WIDTH)]
    grads = mm3(split(jnp.transpose(dqkv_ref[3])), split(jnp.concatenate(cots, axis=1)))
    for s in range(D // WIDTH):
        part = along(head_ref[0] + (D // WIDTH - s))[0]
        put(3 * (D // WIDTH) + part, grads[:, s * WIDTH : (s + 1) * WIDTH])


def rows_kernel(dqkv_ref, win_ref, dx_ref, done_ref):
    done_ref[...] = jnp.zeros_like(done_ref)
    grads = split(jnp.concatenate([dqkv_ref[t] for t in range(3)], axis=1))
    for part in range(D // WIDTH):
        rows = slice(part * WIDTH, (part + 1) * WIDTH)
        win = jnp.concatenate([win_ref[t, rows] for t in range(3)], axis=1)
        dx_ref[part] = mm3(grads, split(win), NT)


def call(kernel, outs, *args, scratch=(), sems=(), scalars=0, held=0, sent=0, room=8, flops=10**9):
    size = sum(math.prod(a.shape) * 4 for a in (*args, *outs))
    vmem = pl.BlockSpec(memory_space=pltpu.VMEM)
    hbm = pl.BlockSpec(memory_space=pltpu.HBM)
    return pl.pallas_call(
        kernel,
        out_shape=tuple(jax.ShapeDtypeStruct(o, F32) for o in [x.shape for x in outs]),
        in_specs=[pl.BlockSpec(memory_space=pltpu.SMEM)] * scalars
        + [hbm] * held
        + [vmem] * (len(args) - scalars - held),
        out_specs=tuple([hbm] * sent + [vmem] * (len(outs) - sent)),
        scratch_shapes=[pltpu.VMEM(x, F32) if isinstance(x, tuple) else x for x in scratch]
        + [pltpu.SemaphoreType.DMA(n) for n in sems],
        compiler_params=pltpu.CompilerParams(vmem_limit_bytes=room * 2**20),
        cost_estimate=pl.CostEstimate(flops=flops, bytes_accessed=size, transcendentals=0),
    )(*args)


def of(*shape):
    return jax.ShapeDtypeStruct(shape, F32)


def swap(x, axis):
    return lax.all_to_all(x, axis, split_axis=0, concat_axis=0, tiled=True)


def shards(features, input_proj, output_proj, destination, real_points, cotangent):
    peers = lax.axis_size(CURVE)
    each = PATCH // peers
    up = [(i, (i + 1) % peers) for i in range(peers)]
    down = [(j, i) for i, j in up]
    heads = lax.axis_size("head")
    head = lax.axis_index("head").astype(jnp.int32).reshape(1)
    core = lax.axis_index("core").astype(jnp.int32).reshape(1)

    def ahead(x, step):
        return lax.ppermute(x, "head", [(i, (i + step) % heads) for i in range(heads)])

    def exchange(message):
        rows = message.shape[0]
        return swap(message.reshape(rows, 1, WIDTH), CURVE).reshape(rows, WIDTH)

    index, lists = call(
        functools.partial(index_kernel, each), [of(1, PATCH), of(peers, WIDTH)], destination.reshape(1, PATCH)
    )
    (message,) = call(functools.partial(sort_kernel, each), [of(PATCH + peers, WIDTH)], index, lists, features)
    arrived = exchange(message)
    cots = [cotangent] + [ahead(cotangent, s) for s in (1, 2, 3)]
    win = jnp.transpose(input_proj, (1, 0, 2))
    valid = jnp.concatenate([lax.ppermute(real_points[HALF:], CURVE, up), real_points[:HALF]], axis=0)
    valid = valid.reshape(1, PATCH)
    low, high, position = call(
        functools.partial(place_kernel, each),
        [of(HALF, WIDTH), of(HALF, WIDTH), of(1, PATCH)], *cots[1:], arrived, held=3,
    )
    grad_early, grad_late, cot_early, cot_late = call(
        cot_kernel, [of(HALF, WIDTH)] * 2 + [of(heads, HALF, WIDTH)] * 2, head, *cots, output_proj, scalars=1,
    )
    grad_before = lax.ppermute(grad_late, CURVE, up)
    before = lax.ppermute(cot_late, CURVE, up)
    x = jnp.concatenate([lax.ppermute(high, CURVE, up), low], axis=0)
    x = jnp.broadcast_to(x[None], (D // WIDTH, PATCH, WIDTH))
    x, grad_early = lax.optimization_barrier((x, grad_early))
    x = swap(x.reshape(-1, WIDTH), "head").reshape(D // WIDTH, PATCH, WIDTH)
    qkv, attended, lse = call(
        forward_kernel,
        [of(3, PATCH, WIDTH), of(WIDTH, PATCH), of(HERE, PATCH)],
        x, win, valid, scratch=[(WIDTH, PATCH)] + [(HERE, PATCH, WIDTH)] * 2, room=24,
    )
    (dqkv,) = call(
        backward_kernel, [of(4, PATCH, WIDTH)], qkv, attended, lse, grad_before, grad_early, valid,
        scratch=[(WIDTH, PATCH)] * 3 + [(PATCH, WIDTH)] + [(HERE, PATCH, WIDTH)] * 4, room=24,
    )
    dx, done = call(
        rows_kernel, [of(D // WIDTH, PATCH, WIDTH), of(8, WIDTH)], dqkv, win
    )
    dx = swap(dx.reshape(-1, WIDTH), "head").reshape(D // WIDTH, PATCH, WIDTH)
    dx_early, dx_late = call(add_kernel, [of(HALF, WIDTH)] * 2, dx)
    keep, send = call(
        weights_kernel, [of(BLOCKS, SIDE, WIDTH)] * 2, core, head, x, dqkv, before, cot_early, done, scalars=2
    )
    out = call(output_kernel, [of(PATCH, WIDTH)] * heads, head, attended, output_proj, done, scalars=1)
    out = [out[0]] + [ahead(out[s], s) for s in (1, 2, 3)]
    out_early, out_late = call(sum_kernel, [of(HALF, WIDTH)] * 2, *out)
    sums = keep + lax.ppermute(send, "core", [(0, 1), (1, 0)])
    sums, dx_early = lax.optimization_barrier((sums, dx_early))
    sums = swap(sums.reshape(-1, WIDTH), PLANE).reshape(BLOCKS, SIDE, WIDTH)
    (message,) = call(
        functools.partial(pack_kernel, each), [of(peers * (each + ADDED), WIDTH)],
        position, dx_late, lax.ppermute(dx_early, CURVE, down), sums,
    )
    message = exchange(message)
    (sums,) = call(
        functools.partial(unpack_kernel, each), [of(BLOCKS, SIDE, WIDTH)], message,
        sent=1, scratch=[(SIDE, WIDTH)], sems=[(BLOCKS,)],
    )
    sums, out_early = lax.optimization_barrier((sums, out_early))
    sums = swap(sums.reshape(-1, WIDTH), PLANE).reshape(BLOCKS, SIDE, WIDTH)
    branch_out = jnp.concatenate([out_late, lax.ppermute(out_early, CURVE, down)], axis=0)
    sums, message, branch_out = lax.optimization_barrier((sums, message, branch_out))
    (grad_features,) = call(functools.partial(unsort_kernel, each), [of(PATCH, WIDTH)], index, message)
    grad_inproj, grad_outproj = call(
        finish_kernel, [of(3, D, WIDTH), of(WIDTH, D)],
        core, sums, lax.ppermute(sums, "core", [(0, 1), (1, 0)]), scalars=1,
    )
    return (branch_out, grad_features, jnp.transpose(grad_inproj, (1, 0, 2)), grad_outproj)


def solution(mesh):
    curve, head = mesh.devices.shape
    sizes = (curve // 32, 4, 4, 2)
    fine = jax.sharding.Mesh(mesh.devices.reshape(*sizes, head), CURVE + ("head",))
    return jax.shard_map(
        shards,
        mesh=fine,
        in_specs=(
            P(CURVE, "head"),
            P(None, None, "head"),
            P("head", None),
            P(CURVE),
            P(CURVE),
            P(CURVE, "head"),
        ),
        out_specs=(P(CURVE, "head"), P(CURVE, "head"), P(None, None, "head"), P("head", None)),
        check_vma=False,
    )
```

```python
import functools
import math

import jax
import jax.numpy as jnp
from jax import lax
from jax.experimental import pallas as pl
from jax.experimental.pallas import tpu as pltpu
from jax.sharding import PartitionSpec as P

D = 512
HEADS = 16
PATCH = 512
HALF = PATCH // 2
HEAD = D // HEADS
WIDTH = 128
HERE = WIDTH // HEAD
CURVE = ("far", "near", "x", "core")
PLANE = ("near", "x")
BLOCKS = 16
SIDE = WIDTH // 2
ADDED = 2
BF = jnp.bfloat16
F32 = jnp.float32
SCALE = 1.0 / math.sqrt(HEAD)
LOG2E = math.log2(math.e)

NN = (((1,), (0,)), ((), ()))
NT = (((1,), (1,)), ((), ()))


def mm(a, b, dims=NN):
    return lax.dot_general(a, b, dims, preferred_element_type=F32)


def split(x):
    high = x.astype(BF)
    return high, (x - high.astype(F32)).astype(BF)


def split3(x):
    high, rest = x.astype(BF), None
    rest = x - high.astype(F32)
    mid = rest.astype(BF)
    return high, mid, (rest - mid.astype(F32)).astype(BF)


def mm3(a, b, dims=NN):
    (ah, al), (bh, bl) = a, b
    (left,), (right,) = dims[0]
    return mm(jnp.concatenate([ah, al, ah], axis=left), jnp.concatenate([bh, bh, bl], axis=right), dims)


def select_rows(pick, x):
    high, mid, low = split3(x)
    return mm(pick, high) + (mm(pick, mid) + mm(pick, low))


def column(row):
    return jnp.transpose(jnp.broadcast_to(row, (WIDTH, row.shape[1])))


def wide(col, width=PATCH):
    return jnp.concatenate([col] * (width // WIDTH), axis=1)


def iota(dim, shape=(PATCH, PATCH)):
    return lax.broadcasted_iota(jnp.int32, shape, dim).astype(F32)


def one_hot(condition):
    return jnp.where(condition, 1.0, 0.0).astype(BF)


def every(ref, first, step):
    return ref[pl.ds(first, ref.shape[0] // step, stride=step), :]


def index_kernel(each, dest_ref, index_ref, lists_ref):
    peers = PATCH // each
    dest = dest_ref[...]
    block = dest // PATCH
    local = (dest - block * PATCH).astype(F32)
    block = block.astype(F32)
    same = (wide(column(block)) == block) & (iota(0) < iota(1))
    rank = jnp.sum(jnp.where(same, 1.0, 0.0), axis=0, keepdims=True)
    index_ref[...] = rank * peers + block
    high, low = split(jnp.where(iota(1, (PATCH, WIDTH)) == column(rank), column(local), 0.0))
    mine = one_hot(iota(0, (peers, PATCH)) == block)
    lists_ref[...] = mm(mine, high) + mm(mine, low)


def sort_kernel(each, index_ref, lists_ref, feat_ref, message_ref):
    peers = PATCH // each
    rows = select_rows(one_hot(iota(0) == index_ref[...]), feat_ref[...])
    for turn in range(each):
        message_ref[pl.ds(turn, peers, stride=each + 1), :] = rows[turn * peers : (turn + 1) * peers]
    message_ref[pl.ds(each, peers, stride=each + 1), :] = lists_ref[...]


def place_kernel(each, after1_ref, after2_ref, after3_ref, after4_ref, message_ref, low_ref, high_ref, position_ref):
    del after1_ref, after2_ref, after3_ref, after4_ref
    turned = jnp.transpose(every(message_ref, each, each + 1))
    position = jnp.concatenate([turned[turn : turn + 1] for turn in range(each)], axis=1)
    position_ref[...] = position
    arrived = jnp.concatenate([every(message_ref, turn, each + 1) for turn in range(each)], axis=0)
    placed = select_rows(one_hot(iota(0) == position), arrived)
    low_ref[...] = placed[:HALF]
    high_ref[...] = placed[HALF:]


def add_kernel(parts_ref, early_ref, late_ref):
    total = parts_ref[0] + parts_ref[1] + (parts_ref[2] + parts_ref[3])
    early_ref[...] = total[:HALF]
    late_ref[...] = total[HALF:]


def pack_kernel(each, position_ref, low_ref, high_ref, sums_ref, message_ref):
    peers = PATCH // each
    size = each + ADDED
    grads = jnp.concatenate([low_ref[...], high_ref[...]], axis=0)
    rows = select_rows(one_hot(wide(column(position_ref[...])) == iota(1)), grads)
    for turn in range(each):
        message_ref[pl.ds(turn, peers, stride=size), :] = rows[turn * peers : (turn + 1) * peers]
    sums = sums_ref[0]
    for part in range(1, sums_ref.shape[0]):
        sums += sums_ref[part]
    near = SIDE // ADDED
    for turn in range(ADDED):
        for core in range(2):
            first = turn * near + core * BLOCKS
            rows = jnp.concatenate([sums[first : first + BLOCKS]] * (peers // near), axis=0)
            message_ref[pl.ds(core * size + each + turn, peers // 2, stride=2 * size), :] = rows


def unpack_kernel(each, message_ref, out_hbm, sums_ref, sems):
    near = SIDE // ADDED
    for turn in range(ADDED):
        rows = every(message_ref, each + turn, each + ADDED)
        total = rows[:near]
        for far in range(1, rows.shape[0] // near):
            total += rows[far * near : (far + 1) * near]
        sums_ref[turn * near : (turn + 1) * near] = total
    copies = [pltpu.make_async_copy(sums_ref, out_hbm.at[i], sems.at[i]) for i in range(BLOCKS)]
    for copy in copies:
        copy.start()
    for copy in copies:
        copy.wait()


def unsort_kernel(each, index_ref, message_ref, out_ref):
    returned = jnp.concatenate([every(message_ref, turn, each + ADDED) for turn in range(each)], axis=0)
    out_ref[...] = select_rows(one_hot(wide(column(index_ref[...])) == iota(1)), returned)


def finish_kernel(core_ref, mine_ref, other_ref, din_ref, dout_ref):
    core = core_ref[0]
    near = SIDE // ADDED
    for own, ref in ((core, mine_ref), (1 - core, other_ref)):
        for block in range(BLOCKS):
            t, part = divmod(block, D // WIDTH)
            for side in range(2):
                for turn in range(ADDED):
                    got = ref[:, turn * near + 2 * block + side, :]
                    first = pl.multiple_of(side * SIDE + turn * near + own * BLOCKS, BLOCKS)
                    if t < 3:
                        din_ref[t, pl.ds(part * WIDTH + first, BLOCKS), :] = got
                    else:
                        dout_ref[pl.ds(first, BLOCKS), part * WIDTH : (part + 1) * WIDTH] = got


def head_mask(head):
    lanes = lax.broadcasted_iota(jnp.int32, (PATCH, WIDTH), 1)
    return (lanes // HEAD) == head


def turned(x, order):
    high, low = split(x)
    parts = {"h": high.astype(F32), "l": low.astype(F32)}
    return [parts[o] if not i else pltpu.roll(parts[o], i * HEAD, 1) for i, o in enumerate(order)]


def of_head(refs, head):
    lanes = lax.broadcasted_iota(jnp.int32, (PATCH, WIDTH), 1)
    turn = (lanes // HEAD - head) & (HERE - 1)
    x = refs[0]
    for i in range(1, HERE):
        x = jnp.where(turn == i, refs[i], x)
    return x.astype(BF)


def keep(ref, parts):
    for i, part in enumerate(parts):
        ref[i] = part


def forward_kernel(x_ref, win_ref, valid_ref, qkv_ref, att_ref, lse_ref, vt_ref, q_ref, k_ref):
    x = jnp.concatenate([x_ref[part] for part in range(D // WIDTH)], axis=1)
    win = jnp.concatenate([win_ref[t] for t in range(3)], axis=1)
    qkv = mm3(split(x), split(win))
    for t in range(3):
        qkv_ref[t] = qkv[:, t * WIDTH : (t + 1) * WIDTH]
    vt_ref[...] = jnp.transpose(qkv_ref[2])
    keep(q_ref, turned(qkv_ref[0] * (SCALE * LOG2E), "hhll"))
    keep(k_ref, turned(qkv_ref[1], "hlhl"))
    bias = wide(column(jnp.where(valid_ref[...] > 0, 0.0, -jnp.inf)))

    def one(head, carry):
        scores = mm(of_head(k_ref, head), of_head(q_ref, head), NT) + bias
        top = jnp.max(scores, axis=0, keepdims=True)
        weights = jnp.exp2(scores - top)
        total = jnp.sum(weights, axis=0, keepdims=True)
        rows = pl.ds(pl.multiple_of(head * HEAD, HEAD), HEAD)
        vh, vl = split(vt_ref[rows, :])
        wh, wl = split(weights)
        both = mm(jnp.concatenate([vh, vl], axis=0), wh)
        attended = both[:HEAD] + both[HEAD:] + mm(vh, wl)
        att_ref[rows, :] = attended / total
        lse_ref[pl.ds(head, 1), :] = top + jnp.log2(total)
        return carry

    lax.fori_loop(0, HERE, one, 0, unroll=True)


def cot_kernel(head_ref, cot_ref, cot1_ref, cot2_ref, cot3_ref, wout_ref, early_ref, late_ref, stay_ref, send_ref):
    cots = [ref[...] for ref in (cot_ref, cot1_ref, cot2_ref, cot3_ref)]
    wout = [wout_ref[:, along(head_ref[0] + (D // WIDTH - s))[1]] for s in range(D // WIDTH)]
    grads = mm3(split(jnp.concatenate(cots, axis=1)), split(jnp.concatenate(wout, axis=1)), NT)
    early_ref[...] = grads[:HALF]
    late_ref[...] = grads[HALF:]
    for s, cot in enumerate(cots):
        stay_ref[s] = cot[:HALF]
        send_ref[s] = cot[HALF:]


def along(step):
    part = lax.rem(step, D // WIDTH)
    return part, pl.ds(pl.multiple_of(part * WIDTH, WIDTH), WIDTH)


def output_kernel(head_ref, att_ref, wout_ref, after_ref, *out_refs):
    del after_ref
    attended = split(jnp.transpose(att_ref[...]))
    for step, out_ref in enumerate(out_refs):
        out_ref[...] = mm3(attended, split(wout_ref[:, along(head_ref[0] + step)[1]]))


def sum_kernel(first_ref, second_ref, third_ref, fourth_ref, early_ref, late_ref):
    total = first_ref[...] + second_ref[...] + (third_ref[...] + fourth_ref[...])
    early_ref[...] = total[:HALF]
    late_ref[...] = total[HALF:]


def backward_kernel(
    qkv_ref, att_ref, lse_ref, before_ref, early_ref, valid_ref,
    dqkv_ref, kt_ref, gt_ref, dqt_ref, grad_ref, q_ref, k_ref, v_ref, g_ref,
):
    grad_ref[:HALF] = before_ref[...]
    grad_ref[HALF:] = early_ref[...]
    kt_ref[...] = jnp.transpose(qkv_ref[1])
    gt_ref[...] = jnp.transpose(grad_ref[...])
    keep(q_ref, turned(qkv_ref[0] * (SCALE * LOG2E), "hhll"))
    keep(k_ref, turned(qkv_ref[1], "hlhl"))
    keep(g_ref, turned(grad_ref[...], "hhll"))
    keep(v_ref, turned(qkv_ref[2], "hlhl"))
    bias = wide(column(jnp.where(valid_ref[...] > 0, 0.0, -jnp.inf)))
    dqkv_ref[1] = jnp.zeros((PATCH, WIDTH), F32)
    dqkv_ref[2] = jnp.zeros((PATCH, WIDTH), F32)

    def one(head, carry):
        mask = head_mask(head)
        rows = pl.ds(pl.multiple_of(head * HEAD, HEAD), HEAD)
        scores = mm(of_head(k_ref, head), of_head(q_ref, head), NT) + bias
        probs = jnp.exp2(scores - lse_ref[pl.ds(head, 1), :])
        ph, plo = split(probs)
        grad_probs = mm(of_head(v_ref, head), of_head(g_ref, head), NT)
        gh, gl = split(jnp.where(mask, grad_ref[...], 0.0))
        both = mm(ph, jnp.concatenate([gh, gl], axis=1))
        dqkv_ref[2] += both[:, :WIDTH] + both[:, WIDTH:] + mm(plo, gh)
        inner = jnp.sum(gt_ref[rows, :] * att_ref[rows, :], axis=0, keepdims=True)
        grad_scores = probs * (grad_probs - inner)
        sh, sl = split(grad_scores)
        qh, ql = split(jnp.where(mask, qkv_ref[0] * SCALE, 0.0))
        both = mm(sh, jnp.concatenate([qh, ql], axis=1))
        dqkv_ref[1] += both[:, :WIDTH] + both[:, WIDTH:] + mm(sl, qh)
        kh, kl = split(kt_ref[rows, :] * SCALE)
        both = mm(jnp.concatenate([kh, kl], axis=0), sh)
        dqt_ref[rows, :] = both[:HEAD] + both[HEAD:] + mm(kh, sl)
        return carry

    lax.fori_loop(0, HERE, one, 0, unroll=True)
    dqkv_ref[0] = jnp.transpose(dqt_ref[...])
    dqkv_ref[3] = jnp.transpose(att_ref[...])


def weights_kernel(core_ref, head_ref, x_ref, dqkv_ref, before_ref, early_ref, after_ref, keep_ref, send_ref):
    del after_ref
    second = core_ref[0] == 1

    def put(block, grads):
        top, bottom = grads[:SIDE], grads[SIDE:]
        keep_ref[block] = jnp.where(second, bottom, top)
        send_ref[block] = jnp.where(second, top, bottom)

    x = split(jnp.concatenate([x_ref[part] for part in range(D // WIDTH)], axis=1))
    for t in range(3):
        grads = jnp.transpose(mm3(split(jnp.transpose(dqkv_ref[t])), x))
        for part in range(D // WIDTH):
            put(t * (D // WIDTH) + part, grads[part * WIDTH : (part + 1) * WIDTH])
    cots = [jnp.concatenate([before_ref[s], early_ref[s]], axis=0) for s in range(D // WIDTH)]
    grads = mm3(split(jnp.transpose(dqkv_ref[3])), split(jnp.concatenate(cots, axis=1)))
    for s in range(D // WIDTH):
        part = along(head_ref[0] + (D // WIDTH - s))[0]
        put(3 * (D // WIDTH) + part, grads[:, s * WIDTH : (s + 1) * WIDTH])


def rows_kernel(dqkv_ref, win_ref, dx_hbm, done_ref, dx_ref, sems):
    done_ref[...] = jnp.zeros_like(done_ref)
    grads = split(jnp.concatenate([dqkv_ref[t] for t in range(3)], axis=1))
    copies = []
    for part in range(D // WIDTH):
        rows = slice(part * WIDTH, (part + 1) * WIDTH)
        win = jnp.concatenate([win_ref[t, rows] for t in range(3)], axis=1)
        dx_ref[part] = mm3(grads, split(win), NT)
        copies.append(pltpu.make_async_copy(dx_ref.at[part], dx_hbm.at[part], sems.at[part]))
        copies[-1].start()
    for copy in copies:
        copy.wait()


def call(kernel, outs, *args, scratch=(), sems=(), scalars=0, held=0, sent=0, room=8, flops=10**9):
    size = sum(math.prod(a.shape) * 4 for a in (*args, *outs))
    vmem = pl.BlockSpec(memory_space=pltpu.VMEM)
    hbm = pl.BlockSpec(memory_space=pltpu.HBM)
    return pl.pallas_call(
        kernel,
        out_shape=tuple(jax.ShapeDtypeStruct(o, F32) for o in [x.shape for x in outs]),
        in_specs=[pl.BlockSpec(memory_space=pltpu.SMEM)] * scalars
        + [hbm] * held
        + [vmem] * (len(args) - scalars - held),
        out_specs=tuple([hbm] * sent + [vmem] * (len(outs) - sent)),
        scratch_shapes=[pltpu.VMEM(x, F32) if isinstance(x, tuple) else x for x in scratch]
        + [pltpu.SemaphoreType.DMA(n) for n in sems],
        compiler_params=pltpu.CompilerParams(vmem_limit_bytes=room * 2**20),
        cost_estimate=pl.CostEstimate(flops=flops, bytes_accessed=size, transcendentals=0),
    )(*args)


def of(*shape):
    return jax.ShapeDtypeStruct(shape, F32)


def swap(x, axis):
    return lax.all_to_all(x, axis, split_axis=0, concat_axis=0, tiled=True)


def shards(features, input_proj, output_proj, destination, real_points, cotangent):
    peers = lax.axis_size(CURVE)
    each = PATCH // peers
    up = [(i, (i + 1) % peers) for i in range(peers)]
    down = [(j, i) for i, j in up]
    heads = lax.axis_size("head")
    head = lax.axis_index("head").astype(jnp.int32).reshape(1)
    core = lax.axis_index("core").astype(jnp.int32).reshape(1)

    def ahead(x, step):
        return lax.ppermute(x, "head", [(i, (i + step) % heads) for i in range(heads)])

    def exchange(message):
        rows = message.shape[0]
        return swap(message.reshape(rows, 1, WIDTH), CURVE).reshape(rows, WIDTH)

    index, lists = call(
        functools.partial(index_kernel, each), [of(1, PATCH), of(peers, WIDTH)], destination.reshape(1, PATCH)
    )
    (message,) = call(functools.partial(sort_kernel, each), [of(PATCH + peers, WIDTH)], index, lists, features)
    arrived = exchange(message)
    cots = [cotangent] + [ahead(cotangent, s) for s in (1, 2, 3)]
    win = jnp.transpose(input_proj, (1, 0, 2))
    valid = jnp.concatenate([lax.ppermute(real_points[HALF:], CURVE, up), real_points[:HALF]], axis=0)
    valid = valid.reshape(1, PATCH)
    low, high, position = call(
        functools.partial(place_kernel, each),
        [of(HALF, WIDTH), of(HALF, WIDTH), of(1, PATCH)], *cots[1:], valid, arrived, held=4,
    )
    grad_early, grad_late, cot_early, cot_late = call(
        cot_kernel, [of(HALF, WIDTH)] * 2 + [of(heads, HALF, WIDTH)] * 2, head, *cots, output_proj, scalars=1,
    )
    grad_before = lax.ppermute(grad_late, CURVE, up)
    before = lax.ppermute(cot_late, CURVE, up)
    x = jnp.concatenate([lax.ppermute(high, CURVE, up), low], axis=0)
    x = jnp.broadcast_to(x[None], (D // WIDTH, PATCH, WIDTH))
    x, grad_early = lax.optimization_barrier((x, grad_early))
    x = swap(x.reshape(-1, WIDTH), "head").reshape(D // WIDTH, PATCH, WIDTH)
    qkv, attended, lse = call(
        forward_kernel,
        [of(3, PATCH, WIDTH), of(WIDTH, PATCH), of(HERE, PATCH)],
        x, win, valid, scratch=[(WIDTH, PATCH)] + [(HERE, PATCH, WIDTH)] * 2, room=24,
    )
    (dqkv,) = call(
        backward_kernel, [of(4, PATCH, WIDTH)], qkv, attended, lse, grad_before, grad_early, valid,
        scratch=[(WIDTH, PATCH)] * 3 + [(PATCH, WIDTH)] + [(HERE, PATCH, WIDTH)] * 4, room=24,
    )
    dx, done = call(
        rows_kernel, [of(D // WIDTH, PATCH, WIDTH), of(8, WIDTH)], dqkv, win,
        sent=1, scratch=[(D // WIDTH, PATCH, WIDTH)], sems=[(D // WIDTH,)],
    )
    dx = swap(dx.reshape(-1, WIDTH), "head").reshape(D // WIDTH, PATCH, WIDTH)
    dx_early, dx_late = call(add_kernel, [of(HALF, WIDTH)] * 2, dx)
    keep, send = call(
        weights_kernel, [of(BLOCKS, SIDE, WIDTH)] * 2, core, head, x, dqkv, before, cot_early, done, scalars=2
    )
    out = call(output_kernel, [of(PATCH, WIDTH)] * heads, head, attended, output_proj, done, scalars=1)
    out = [out[0]] + [ahead(out[s], s) for s in (1, 2, 3)]
    out_early, out_late = call(sum_kernel, [of(HALF, WIDTH)] * 2, *out)
    sums = keep + lax.ppermute(send, "core", [(0, 1), (1, 0)])
    sums, dx_early = lax.optimization_barrier((sums, dx_early))
    sums = swap(sums.reshape(-1, WIDTH), PLANE).reshape(BLOCKS, SIDE, WIDTH)
    (message,) = call(
        functools.partial(pack_kernel, each), [of(peers * (each + ADDED), WIDTH)],
        position, dx_late, lax.ppermute(dx_early, CURVE, down), sums,
    )
    message = exchange(message)
    (sums,) = call(
        functools.partial(unpack_kernel, each), [of(BLOCKS, SIDE, WIDTH)], message,
        sent=1, scratch=[(SIDE, WIDTH)], sems=[(BLOCKS,)],
    )
    sums, out_early = lax.optimization_barrier((sums, out_early))
    sums = swap(sums.reshape(-1, WIDTH), PLANE).reshape(BLOCKS, SIDE, WIDTH)
    branch_out = jnp.concatenate([out_late, lax.ppermute(out_early, CURVE, down)], axis=0)
    sums, message, branch_out = lax.optimization_barrier((sums, message, branch_out))
    (grad_features,) = call(functools.partial(unsort_kernel, each), [of(PATCH, WIDTH)], index, message)
    grad_inproj, grad_outproj = call(
        finish_kernel, [of(3, D, WIDTH), of(WIDTH, D)],
        core, sums, lax.ppermute(sums, "core", [(0, 1), (1, 0)]), scalars=1,
    )
    return (branch_out, grad_features, jnp.transpose(grad_inproj, (1, 0, 2)), grad_outproj)


def solution(mesh):
    curve, head = mesh.devices.shape
    sizes = (curve // 32, 4, 4, 2)
    fine = jax.sharding.Mesh(mesh.devices.reshape(*sizes, head), CURVE + ("head",))
    return jax.shard_map(
        shards,
        mesh=fine,
        in_specs=(
            P(CURVE, "head"),
            P(None, None, "head"),
            P("head", None),
            P(CURVE),
            P(CURVE),
            P(CURVE, "head"),
        ),
        out_specs=(P(CURVE, "head"), P(CURVE, "head"), P(None, None, "head"), P("head", None)),
        check_vma=False,
    )
```
